256 devices in a mesh: row: 16 (over z_lo, x, core), col: 16 (over y, z_hi).
Axes of the slice: x: 4, y: 4, z: 8 (z_hi: 4, z_lo: 2; z = z_hi * 2 + z_lo), core: 2. Of those that a mesh axis runs over, the one named last changes fastest.
Arguments:
- pool: bfloat16 [16384, 1024], P(('row', 'col')), may hold values from -16 to 16
- targets: bfloat16 [16384, 1024], P(('row', 'col')), may hold values from -16 to 16
- counts: int32 [16384], P(('row', 'col')), may hold values from 0 to 7, as said below
Outputs:
- proof: float32 [16384], P(('row', 'col'))
- gradient: float32 [16384, 1024], P(('row', 'col'))
The draws below stay inside these ranges and needn't reach their ends.
Inputs may be any that keep to these rules, and one draw needn't show every extreme that they name: `counts`: counts of selections; the last pool example has count 7.
All inputs are finite; a program needn't handle non-finite values.
Results may differ from the reference program's by a relative error of at most 0.0014.
Values may be sent and summed in bfloat16 or wider, within the bound.
No kernel may reach another device: no remote copies, remote signals or barrier semaphores. Data moves between devices by JAX's collectives and lax.ppermute only.
A program may use at most 64 MiB of HBM per device.

```python
import math
import jax
import jax.numpy as jnp
from jax import lax

D = 1024
POOL = 16384
TARGETS = 16384


def centre_table(key):
    centre_count = max(POOL // 32, 4)
    base = jax.random.fold_in(key, 9001)
    key_common, key_level, key_spread, key_own = jax.random.split(base, 4)
    common = jax.random.truncated_normal(key_common, -4.0, 4.0, (D,), jnp.float32)
    level = jax.random.uniform(key_level, (centre_count,), jnp.float32, -1.5, 1.5)
    spread = jnp.exp(jax.random.uniform(key_spread, (centre_count,), jnp.float32, math.log(0.3), math.log(1.5)))
    own = jax.random.truncated_normal(key_own, -4.0, 4.0, (centre_count, D), jnp.float32) * spread[:, None]
    return level[:, None] * common[None, :] + own


def draw_examples(key, number, choosable, table):
    key_which, key_scale, key_noise = jax.random.split(key, 3)
    which = jax.random.randint(key_which, (number,), 0, choosable, dtype=jnp.int32)
    scale = jnp.exp(jax.random.uniform(key_scale, (number,), jnp.float32, math.log(0.3), math.log(0.8)))
    noise = jax.random.truncated_normal(key_noise, -4.0, 4.0, (number, D), jnp.float32)
    rows = table[which] + noise * scale[:, None]
    return jnp.clip(rows, -16.0, 16.0).astype(jnp.bfloat16)


def draw_pool(key, part):
    table = centre_table(key)
    return draw_examples(jax.random.fold_in(key, 11), POOL, table.shape[0], table)


def draw_targets(key, part):
    table = centre_table(key)
    return draw_examples(jax.random.fold_in(key, 12), TARGETS, table.shape[0] // 2, table)


def draw_counts(key, part):
    position = jnp.arange(POOL, dtype=jnp.int32)
    ceiling = 1 + 7 * position // POOL
    raw = jax.random.randint(key, (POOL,), 0, 8, dtype=jnp.int32)
    capped = jnp.minimum(raw, ceiling)
    return jnp.where(position == POOL - 1, ceiling, capped).astype(jnp.int32)


def setup_inputs(seed: int = 0) -> dict:
    key_list = jax.random.split(jax.random.key(seed), 4)
    pool = draw_pool(jax.random.fold_in(key_list[3], 71), 0)
    targets = draw_targets(jax.random.fold_in(key_list[3], 71), 0)
    counts = draw_counts(jax.random.fold_in(key_list[3], 71), 0)
    return dict(pool=pool, targets=targets, counts=counts)


def kernel_tile(row_panel, row_norms, columns):
    col_float = columns.astype(jnp.float32)
    col_norms = jnp.sum(col_float * col_float, axis=1)
    inner = jnp.dot(row_panel, columns.T, preferred_element_type=jnp.float32)
    squared = row_norms[:, None] + col_norms[None, :] - 2.0 * inner
    return jnp.exp(-squared * (0.5 / D))


def reference(pool, targets, counts):
    weights = counts.astype(jnp.float32)
    weight_total = jnp.sum(weights)
    block_rows = math.gcd(POOL, 256)

    def one_block(index_block):
        row_panel = lax.dynamic_slice_in_dim(pool, (index_block * block_rows).astype(jnp.int32), block_rows, 0)
        row_float = row_panel.astype(jnp.float32)
        row_norms = jnp.sum(row_float * row_float, axis=1)
        pool_kernel = kernel_tile(row_panel, row_norms, pool) * weights[None, :]
        target_kernel = kernel_tile(row_panel, row_norms, targets)
        pool_mass = jnp.sum(pool_kernel, axis=1)
        target_mass = jnp.sum(target_kernel, axis=1)
        pool_pull = jnp.dot(pool_kernel.astype(jnp.bfloat16), pool, preferred_element_type=jnp.float32)
        target_pull = jnp.dot(target_kernel.astype(jnp.bfloat16), targets, preferred_element_type=jnp.float32)
        proof = target_mass / TARGETS - pool_mass / weight_total
        gradient = (target_pull - target_mass[:, None] * row_float) / TARGETS - (pool_pull - pool_mass[:, None] * row_float) / weight_total
        return proof, gradient

    proof, gradient = lax.map(one_block, jnp.arange(POOL // block_rows, dtype=jnp.int32))
    return proof.reshape(POOL), gradient.reshape(POOL, D)
```

```python
import functools

import jax
import jax.numpy as jnp
from jax import lax
from jax.experimental import pallas as pl
from jax.experimental.pallas import tpu as pltpu
from jax.sharding import Mesh
from jax.sharding import PartitionSpec as P

AXES = ("zl", "x", "c", "y", "zh")
RING = ("zl", "zh")
LANES = 128
LEVELS = 32767.0
VMEM = pltpu.CompilerParams(vmem_limit_bytes=56 * 1024 * 1024)


def place(z):
    return z % 2 * 4 + z // 2


def from_behind(x, axis, step):
    size = lax.axis_size(axis)
    pairs = [(i, (i + step) % size) for i in range(size)]
    if axis == RING:
        pairs = [(place(i), place(j)) for i, j in pairs]
    return lax.ppermute(x, axis, pairs)


def gathered(x, axis):
    return [x] + [from_behind(x, axis, step) for step in range(1, lax.axis_size(axis))]


def vmem_specs(count):
    return [pl.BlockSpec(memory_space=pltpu.VMEM)] * count


def lane_sums(x):
    total = x[:, :LANES]
    for at in range(LANES, x.shape[1], LANES):
        total = total + x[:, at : at + LANES]
    return total


def square_norms(block):
    wide = block.astype(jnp.float32)
    return jnp.sum(lane_sums(wide * wide), axis=1, keepdims=True)


def add_columns(panel, row_norms, columns, weights, pull, mass, rows):
    cols = columns[...]
    col_norms = jnp.transpose(jnp.broadcast_to(square_norms(cols), (cols.shape[0], LANES)))[:1]
    scale = 0.5 / cols.shape[1]
    for at in range(0, panel.shape[0], rows):
        part = pl.ds(at, rows)
        inner = lax.dot_general(
            panel[part, :], cols, (((1,), (1,)), ((), ())), preferred_element_type=jnp.float32
        )
        squared = row_norms[part, :1] + col_norms - 2.0 * inner
        kernel = jnp.exp(-squared * scale)
        if weights is not None:
            kernel = kernel * weights
        mass[part, :] += lane_sums(kernel)
        pull[part, :] += jnp.dot(
            kernel.astype(jnp.bfloat16), cols, preferred_element_type=jnp.float32
        )


def first_kernel(ring, *refs):
    blocks, refs = refs[:ring], refs[ring:]
    pool_a, pool_b, target_a, target_b, count_a, count_b, panel, norms, pp, tp, pm, tm = refs
    height = blocks[0].shape[0]
    for i, block in enumerate(blocks):
        part = pl.ds(i * height, height)
        panel[part, :] = block[...]
        norms[part, :] = jnp.broadcast_to(square_norms(block[...]), (height, LANES))
    for total in (pp, tp, pm, tm):
        total[...] = jnp.zeros_like(total)
    columns_into((pool_a, pool_b, target_a, target_b, count_a, count_b), panel, norms, pp, tp, pm, tm)


def columns_into(pieces, panel, norms, pp, tp, pm, tm):
    pool_a, pool_b, target_a, target_b, count_a, count_b = pieces
    rows = 256
    for columns, count in ((pool_a, count_a), (pool_b, count_b)):
        add_columns(panel, norms, columns, count[...].astype(jnp.float32), pp, pm, rows)
    for columns in (target_a, target_b):
        add_columns(panel, norms, columns, None, tp, tm, rows)


def next_kernel(*refs):
    pieces, (panel, norms) = refs[:6], refs[6:8]
    totals = refs[12:]
    for old, new in zip(refs[8:12], totals):
        if old is not new:
            new[...] = old[...]
    columns_into(pieces, panel, norms, *totals)


def last_kernel(target_count, ring, *refs):
    pieces, (panel, norms), (pp, tp, pm, tm), total = refs[:6], refs[6:8], refs[8:12], refs[12]
    codes, notes = refs[13 : 13 + ring], refs[13 + ring :]
    columns_into(pieces, panel, norms, pp, tp, pm, tm)
    weight = total[:1, :1]
    height = codes[0].shape[0]
    for i in range(ring):
        part = pl.ds(i * height, height)
        target_mass = jnp.sum(tm[part, :], axis=1, keepdims=True)
        pool_mass = jnp.sum(pm[part, :], axis=1, keepdims=True)
        own = panel[part, :].astype(jnp.float32)
        proof = target_mass / target_count - pool_mass / weight
        term = (tp[part, :] - target_mass * own) * (1.0 / target_count) - (
            pp[part, :] - pool_mass * own
        ) * (1.0 / weight)
        top = jnp.maximum(jnp.max(jnp.abs(term), axis=1, keepdims=True), 1e-30)
        codes[i][...] = jnp.round(term * (LEVELS / top)).astype(jnp.int32).astype(jnp.int16)
        lane = lax.broadcasted_iota(jnp.int32, (height, LANES), 1)
        notes[i][...] = jnp.where(lane == 0, top * (1.0 / LEVELS), proof)


def sum_kernel(ring, *refs):
    codes, notes, (proof, gradient) = refs[:ring], refs[ring : 2 * ring], refs[2 * ring :]
    total, small = 0.0, 0.0
    for code, note in zip(codes, notes):
        total += code[...].astype(jnp.int32).astype(jnp.float32) * note[:, :1]
        small += note[...]
    gradient[...] = total
    proof[...] = small


def shape(dims, dtype):
    return jax.ShapeDtypeStruct(dims, dtype)


def on_device(pool, targets, counts):
    ring = lax.axis_size(RING)
    height, width = pool.shape
    rows = ring * height
    target_count = float(targets.shape[0] * lax.axis_size(AXES))

    pool_x = jnp.concatenate(gathered(pool, "x"), axis=0)
    targets_y = jnp.concatenate(gathered(targets, "y"), axis=0)
    blocks = gathered(pool, RING)
    pool_pieces = gathered(pool_x, "y")
    target_pieces = gathered(targets_y, "x")

    count_x = jnp.concatenate(gathered(counts.reshape(1, height), "x"), axis=1)
    count_pieces = gathered(count_x, "y")
    other_counts = from_behind(jnp.concatenate(count_pieces, axis=0), "c", 1)
    total = sum(jnp.sum(c) for c in count_pieces) + jnp.sum(other_counts)
    total = jnp.broadcast_to(total.astype(jnp.float32), (8, LANES))
    for bit in (1, 2, 4):
        total = total + lax.ppermute(total, RING, [(place(i), place(i ^ bit)) for i in range(ring)])

    def pieces(i):
        return (
            pool_pieces[i],
            from_behind(pool_pieces[i], "c", 1),
            target_pieces[i],
            from_behind(target_pieces[i], "c", 1),
            count_pieces[i],
            other_counts[i : i + 1],
        )

    f32, bf16 = jnp.float32, jnp.bfloat16
    totals = (shape((rows, width), f32),) * 2 + (shape((rows, LANES), f32),) * 2
    columns = 4 * pool_x.shape[0]
    cost = pl.CostEstimate(flops=4 * rows * columns * width, bytes_accessed=8 << 20, transcendentals=rows * columns)
    panel, norms, *state = pl.pallas_call(
        functools.partial(first_kernel, ring),
        out_shape=(shape((rows, width), bf16), shape((rows, LANES), f32), *totals),
        in_specs=vmem_specs(ring + 6),
        out_specs=tuple(vmem_specs(6)),
        compiler_params=VMEM,
        cost_estimate=cost,
        name="first_columns",
    )(*blocks, *pieces(0))
    for i in (1, 2):
        state = pl.pallas_call(
            next_kernel,
            out_shape=totals,
            in_specs=vmem_specs(12),
            out_specs=tuple(vmem_specs(4)),
            input_output_aliases={8: 0, 9: 1, 10: 2, 11: 3},
            compiler_params=VMEM,
            cost_estimate=cost,
            name="next_columns",
        )(*pieces(i), panel, norms, *state)
    sent = pl.pallas_call(
        functools.partial(last_kernel, target_count, ring),
        out_shape=(shape((height, width), jnp.int16),) * ring + (shape((height, LANES), f32),) * ring,
        in_specs=vmem_specs(13),
        out_specs=tuple(vmem_specs(2 * ring)),
        compiler_params=VMEM,
        cost_estimate=cost,
        name="last_columns",
    )(*pieces(3), panel, norms, *state, total)
    codes, notes = list(sent[:ring]), list(sent[ring:])
    for step in range(1, ring):
        codes[step] = from_behind(codes[step], RING, ring - step)
    for step in range(1, ring):
        notes[step] = from_behind(notes[step], RING, ring - step)
    proof, gradient = pl.pallas_call(
        functools.partial(sum_kernel, ring),
        out_shape=(shape((height, LANES), f32), shape((height, width), f32)),
        in_specs=vmem_specs(2 * ring),
        out_specs=tuple(vmem_specs(2)),
        compiler_params=VMEM,
        name="sum_of_terms",
    )(*codes, *notes)
    return proof[:, 1], gradient


def solution(mesh):
    split = Mesh(mesh.devices.reshape(2, 4, 2, 4, 4), AXES)
    return jax.shard_map(
        on_device,
        mesh=split,
        in_specs=(P(AXES, None), P(AXES, None), P(AXES)),
        out_specs=(P(AXES), P(AXES, None)),
        check_vma=False,
    )
```

```python
import functools

import jax
import jax.numpy as jnp
from jax import lax
from jax.experimental import pallas as pl
from jax.experimental.pallas import tpu as pltpu
from jax.sharding import Mesh
from jax.sharding import PartitionSpec as P

AXES = ("zl", "x", "c", "y", "zh")
RING = ("zl", "zh")
PLANE = ("x", "c", "y")
LANES = 128
META = 16
LEVELS = 32767.0
F32, BF16 = jnp.float32, jnp.bfloat16
VMEM = pltpu.CompilerParams(vmem_limit_bytes=56 * 1024 * 1024)


def shape(dims, dtype):
    return jax.ShapeDtypeStruct(dims, dtype)


def in_vmem(body, name, out_shape, flops=0, traffic=1 << 20, scratch=(), **more):
    spec = pl.BlockSpec(memory_space=pltpu.VMEM)

    def call(*args):
        return pl.pallas_call(
            body,
            out_shape=out_shape,
            in_specs=[spec] * len(args),
            out_specs=jax.tree.map(lambda _: spec, out_shape),
            scratch_shapes=scratch,
            compiler_params=VMEM,
            cost_estimate=pl.CostEstimate(flops=flops, bytes_accessed=traffic, transcendentals=0),
            name=name,
            **more,
        )(*args)

    return call


def lane_sums(x):
    total = x[:, :LANES]
    for at in range(LANES, x.shape[1], LANES):
        total = total + x[:, at : at + LANES]
    return total


def square_norms(block):
    wide = block.astype(F32)
    return jnp.sum(lane_sums(wide * wide), axis=1, keepdims=True)


def along_lanes(column):
    return jnp.transpose(jnp.broadcast_to(column, (column.shape[0], LANES)))[:1]


def halves(a, b):
    return jnp.concatenate([a, b], axis=1)


def pack_block(pool, targets, counts, block, copies):
    height = pool.shape[0]
    block[:height, :] = pool[...]
    block[height : 2 * height, :] = targets[...]
    norms = along_lanes(jnp.concatenate([square_norms(pool[...]), square_norms(targets[...])], axis=0))
    high = norms.astype(BF16).astype(F32)
    middle = (norms - high).astype(BF16).astype(F32)
    low = norms - high - middle
    weights = halves(counts[...].astype(F32), jnp.ones((1, height), F32))
    meta = jnp.concatenate([weights, high, middle, low, jnp.zeros((META - 4, LANES), F32)], axis=0)
    block[2 * height :, :] = jnp.concatenate(
        [meta, jnp.zeros((META, block.shape[1] - LANES), F32)], axis=1
    ).astype(BF16)
    for i in range(copies.shape[0]):
        copies[i] = pool[...]


def pack_line(*refs):
    blocks, (piece, chosen) = refs[:-2], refs[-2:]
    count, height = len(blocks), (blocks[0].shape[0] - META) // 2
    for j, block in enumerate(blocks):
        piece[j * height : (j + 1) * height, :] = block[:height, :]
        piece[(count + j) * height : (count + j + 1) * height, :] = block[height : 2 * height, :]
    metas = [block[2 * height :, :LANES].astype(F32) for block in blocks]
    lanes = [meta[:, half : half + height] for half in (0, height) for meta in metas]
    pairs = [halves(a, b) for a, b in zip(lanes[::2], lanes[1::2])]
    width = piece.shape[1] - LANES * len(pairs)
    piece[2 * count * height :, :] = jnp.concatenate(
        [*pairs, jnp.zeros((META, width), F32)], axis=1
    ).astype(BF16)
    total = jnp.zeros((), F32)
    for j in range(count):
        total += jnp.sum(lanes[j][:1])
    chosen[...] = jnp.full(chosen.shape, total, F32)


def kernels_into(panel, norms, pieces, weights, masses, rows):
    ring, height, width = panel.shape
    blocks = rows // height
    for half in range(2):
        for i, piece in enumerate(pieces):
            size = (piece.shape[0] - META) // 2
            at = half * size
            columns = piece[at : at + size, :]
            meta = piece[2 * size :, at : at + size].astype(F32)
            col_norms = meta[1:2] + meta[2:3] + meta[3:4]
            for r in range(ring // blocks):
                part = slice(r * rows, (r + 1) * rows)
                left = panel[r * blocks : (r + 1) * blocks].reshape(rows, width)
                inner = lax.dot_general(
                    left, columns, (((1,), (1,)), ((), ())), preferred_element_type=F32
                )
                squared = norms[part, :1] + col_norms - 2.0 * inner
                kernel = jnp.exp(-squared * (0.5 / width))
                if half == 0:
                    kernel = kernel * meta[:1]
                masses[half][part, :] += lane_sums(kernel)
                weights[half][part, i * size : (i + 1) * size] = kernel.astype(BF16)


def pulled(weights, pieces, half, part):
    size = (pieces[0].shape[0] - META) // 2
    total = None
    for i, piece in enumerate(pieces):
        one = jnp.dot(
            weights[half][part, i * size : (i + 1) * size],
            piece[half * size : (half + 1) * size, :],
            preferred_element_type=F32,
        )
        total = one if total is None else total + one
    return total


def own_columns(rows, lines, panel, *refs):
    pieces, (pp, tp, pm, tm, norms), weights = refs[:lines], refs[lines : lines + 5], refs[lines + 5 :]
    ring, height, _ = panel.shape
    for i in range(ring):
        part = slice(i * height, (i + 1) * height)
        norms[part, :] = jnp.broadcast_to(square_norms(panel[i]), (height, LANES))
    pm[...] = jnp.zeros_like(pm)
    tm[...] = jnp.zeros_like(tm)
    kernels_into(panel, norms, pieces, weights, (pm, tm), rows)
    for at in range(0, ring * height, rows):
        part = slice(at, at + rows)
        pp[part, :] = pulled(weights, pieces, 0, part)
        tp[part, :] = pulled(weights, pieces, 1, part)


def other_columns(rows, lines, target_count, panel, *refs):
    pieces, refs = refs[:lines], refs[lines:]
    pp, tp, pm_old, tm_old, norms, total, coded, pm, tm, *weights = refs
    ring, height, width = panel.shape
    pm[...] = pm_old[...]
    tm[...] = tm_old[...]
    kernels_into(panel, norms, pieces, weights, (pm, tm), rows)
    weight = total[:1, :1]
    for at in range(0, ring * height, rows):
        part = slice(at, at + rows)
        pool_pull = pp[part, :] + pulled(weights, pieces, 0, part)
        target_pull = tp[part, :] + pulled(weights, pieces, 1, part)
        pool_mass = jnp.sum(pm[part, :], axis=1, keepdims=True)
        target_mass = jnp.sum(tm[part, :], axis=1, keepdims=True)
        own = panel[at // height : (at + rows) // height].reshape(rows, width).astype(F32)
        proof = target_mass / target_count - pool_mass / weight
        term = (target_pull - target_mass * own) * (1.0 / target_count) - (
            pool_pull - pool_mass * own
        ) * (1.0 / weight)
        code = encode(term, proof)
        for i in range(rows // height):
            coded[at // height + i] = code[i * height : (i + 1) * height, :]


def step_scale(step):
    return jnp.exp2(step * (1.0 / 128.0))


def encode(term, proof):
    top = jnp.maximum(jnp.max(jnp.abs(term), axis=1, keepdims=True), 1e-30)
    step = jnp.ceil(jnp.log2(top) * 128.0)
    steps = jnp.round(term * (LEVELS / step_scale(step)))
    steps = jnp.clip(steps, -LEVELS, LEVELS)
    first = jnp.round(proof * 8192.0)
    rest = (proof * 8192.0 - first) * 32768.0
    second = jnp.round(rest)
    third = jnp.round((rest - second) * 32768.0)
    lane = lax.broadcasted_iota(jnp.int32, (term.shape[0], LANES), 1)
    notes = jnp.where(
        lane == 0, step, jnp.where(lane == 1, first, jnp.where(lane == 2, second, third))
    )
    return jnp.concatenate([steps, notes], axis=1).astype(jnp.int32).astype(jnp.int16)


def add_terms(coded, proof, gradient):
    width = gradient.shape[1]
    total, small = 0.0, 0.0
    for i in range(coded.shape[0]):
        code = coded[i].astype(jnp.int32).astype(F32)
        notes = code[:, width:]
        total += code[:, :width] * (step_scale(notes[:, :1]) * (1.0 / LEVELS))
        parts = notes[:, 1:2], notes[:, 2:3], notes[:, 3:4]
        small += (parts[0] + (parts[1] + parts[2] * (1.0 / 32768.0)) * (1.0 / 32768.0)) * (1.0 / 8192.0)
    gradient[...] = total
    proof[...] = along_lanes(small)


def place(z):
    return z % 2 * 4 + z // 2


def along_line(x, shift, phase):
    pairs = []
    for i in range(4):
        for j in range(4):
            for c in range(2):
                there = (shift(i), j) if (c + phase) % 2 == 0 else (i, shift(j))
                pairs.append(((i * 2 + c) * 4 + j, (there[0] * 2 + c) * 4 + there[1]))
    return lax.ppermute(x, PLANE, pairs)


def line(x, phase):
    return [x] + [along_line(x, lambda i, k=k: (i + k) % 4, phase) for k in (1, 3, 2)]


def other_core(x):
    return lax.ppermute(x, "c", [(0, 1), (1, 0)])


def on_device(pool, targets, counts):
    ring = lax.axis_size(RING)
    height, width = pool.shape
    rows = ring * height
    target_count = float(height * lax.axis_size(AXES))

    block, copies = in_vmem(
        pack_block,
        "pack_block",
        (shape((2 * height + META, width), BF16), shape((ring, height, width), BF16)),
    )(pool, targets, counts.reshape(1, height))
    blocks = line(block, 0)
    panel = lax.all_to_all(copies, RING, split_axis=0, concat_axis=0, tiled=True)
    piece, total = in_vmem(
        pack_line,
        "pack_line",
        (shape((2 * height * len(blocks) + META, width), BF16), shape((8, LANES), F32)),
    )(*blocks)
    pieces = line(piece, 1)
    others = [other_core(p) for p in pieces]

    for bit in (1, 2):
        total = total + along_line(total, lambda i: i ^ bit, 1)
    for bit in (1, 2, 4):
        total = total + lax.ppermute(total, RING, [(place(i), place(i ^ bit)) for i in range(ring)])
    total = total + other_core(total)

    columns = height * len(blocks) * len(pieces)
    flops = 8 * rows * columns * width
    weights = [pltpu.VMEM((rows, columns), BF16)] * 2
    state = in_vmem(
        functools.partial(own_columns, 256, len(pieces)),
        "own_columns",
        (shape((rows, width), F32),) * 2 + (shape((rows, LANES), F32),) * 3,
        flops=flops,
        scratch=weights,
    )(panel, *pieces)
    coded = in_vmem(
        functools.partial(other_columns, 256, len(pieces), target_count),
        "other_columns",
        shape((ring, height, width + LANES), jnp.int16),
        flops=flops,
        scratch=[pltpu.VMEM((rows, LANES), F32)] * 2 + weights,
    )(panel, *others, *state, total)
    coded = lax.all_to_all(coded, RING, split_axis=0, concat_axis=0, tiled=True)
    proof, gradient = in_vmem(
        add_terms, "add_terms", (shape((1, height), F32), shape((height, width), F32))
    )(coded)
    return proof.reshape(height), gradient


def solution(mesh):
    split = Mesh(mesh.devices.reshape(2, 4, 2, 4, 4), AXES)
    return jax.shard_map(
        on_device,
        mesh=split,
        in_specs=(P(AXES, None), P(AXES, None), P(AXES)),
        out_specs=(P(AXES), P(AXES, None)),
        check_vma=False,
    )
```

```python
import functools

import jax
import jax.numpy as jnp
from jax import lax
from jax.experimental import pallas as pl
from jax.experimental.pallas import tpu as pltpu
from jax.sharding import Mesh
from jax.sharding import PartitionSpec as P

AXES = ("zl", "x", "c", "y", "zh")
RING = ("zl", "zh")
PLANE = ("x", "c", "y")
LANES = 128
META = 16
LEVELS = 32767.0
F32, BF16 = jnp.float32, jnp.bfloat16


def shape(dims, dtype):
    return jax.ShapeDtypeStruct(dims, dtype)


def in_vmem(body, name, out_shape, flops=0, traffic=1 << 20, scratch=(), limit=16):
    spec = pl.BlockSpec(memory_space=pltpu.VMEM)

    def call(*args):
        return pl.pallas_call(
            body,
            out_shape=out_shape,
            in_specs=[spec] * len(args),
            out_specs=jax.tree.map(lambda _: spec, out_shape),
            scratch_shapes=scratch,
            compiler_params=pltpu.CompilerParams(vmem_limit_bytes=limit << 20),
            cost_estimate=pl.CostEstimate(flops=flops, bytes_accessed=traffic, transcendentals=0),
            name=name,
        )(*args)

    return call


def lane_sums(x):
    total = x[:, :LANES]
    for at in range(LANES, x.shape[1], LANES):
        total = total + x[:, at : at + LANES]
    return total


def square_norms(block):
    wide = block.astype(F32)
    return jnp.sum(lane_sums(wide * wide), axis=1, keepdims=True)


def along_lanes(column):
    return jnp.transpose(jnp.broadcast_to(column, (column.shape[0], LANES)))[:1]


def halves(a, b):
    return jnp.concatenate([a, b], axis=1)


def pack_block(pool, targets, counts, block, copies):
    height = pool.shape[0]
    block[:height, :] = pool[...]
    block[height : 2 * height, :] = targets[...]
    norms = along_lanes(jnp.concatenate([square_norms(pool[...]), square_norms(targets[...])], axis=0))
    high = norms.astype(BF16).astype(F32)
    middle = (norms - high).astype(BF16).astype(F32)
    low = norms - high - middle
    weights = halves(counts[...].astype(F32), jnp.ones((1, height), F32))
    meta = jnp.concatenate([weights, high, middle, low, jnp.zeros((META - 4, LANES), F32)], axis=0)
    block[2 * height :, :] = jnp.concatenate(
        [meta, jnp.zeros((META, block.shape[1] - LANES), F32)], axis=1
    ).astype(BF16)
    for i in range(copies.shape[0]):
        copies[i] = pool[...]


def pack_line(*refs):
    blocks, (piece, chosen) = refs[:-2], refs[-2:]
    count, height = len(blocks), (blocks[0].shape[0] - META) // 2
    for j, block in enumerate(blocks):
        piece[j * height : (j + 1) * height, :] = block[:height, :]
        piece[(count + j) * height : (count + j + 1) * height, :] = block[height : 2 * height, :]
    metas = [block[2 * height :, :LANES].astype(F32) for block in blocks]
    lanes = [meta[:, half : half + height] for half in (0, height) for meta in metas]
    pairs = [halves(a, b) for a, b in zip(lanes[::2], lanes[1::2])]
    width = piece.shape[1] - LANES * len(pairs)
    piece[2 * count * height :, :] = jnp.concatenate(
        [*pairs, jnp.zeros((META, width), F32)], axis=1
    ).astype(BF16)
    total = jnp.zeros((), F32)
    for j in range(count):
        total += jnp.sum(lanes[j][:1])
    chosen[...] = jnp.full(chosen.shape, total, F32)


def kernels_into(panel, norms, pieces, weights, masses, rows):
    ring, height, width = panel.shape
    blocks = rows // height
    for half in range(2):
        for i, piece in enumerate(pieces):
            size = (piece.shape[0] - META) // 2
            at = half * size
            columns = piece[at : at + size, :]
            meta = piece[2 * size :, at : at + size].astype(F32)
            col_norms = meta[1:2] + meta[2:3] + meta[3:4]
            for r in range(ring // blocks):
                part = slice(r * rows, (r + 1) * rows)
                left = panel[r * blocks : (r + 1) * blocks].reshape(rows, width)
                inner = lax.dot_general(
                    left, columns, (((1,), (1,)), ((), ())), preferred_element_type=F32
                )
                squared = norms[part, :1] + col_norms - 2.0 * inner
                kernel = jnp.exp(-squared * (0.5 / width))
                if half == 0:
                    kernel = kernel * meta[:1]
                masses[half][part, :] += lane_sums(kernel)
                weights[half][part, i * size : (i + 1) * size] = kernel.astype(BF16)


def pulled(weights, pieces, half, part):
    size = (pieces[0].shape[0] - META) // 2
    total = None
    for i, piece in enumerate(pieces):
        one = jnp.dot(
            weights[half][part, i * size : (i + 1) * size],
            piece[half * size : (half + 1) * size, :],
            preferred_element_type=F32,
        )
        total = one if total is None else total + one
    return total


def own_columns(rows, lines, panel, *refs):
    pieces, (pp, tp, pm, tm, norms), weights = refs[:lines], refs[lines : lines + 5], refs[lines + 5 :]
    ring, height, _ = panel.shape
    for i in range(ring):
        part = slice(i * height, (i + 1) * height)
        norms[part, :] = jnp.broadcast_to(square_norms(panel[i]), (height, LANES))
    pm[...] = jnp.zeros_like(pm)
    tm[...] = jnp.zeros_like(tm)
    kernels_into(panel, norms, pieces, weights, (pm, tm), rows)
    for at in range(0, ring * height, rows):
        part = slice(at, at + rows)
        pp[part, :] = pulled(weights, pieces, 0, part)
        tp[part, :] = pulled(weights, pieces, 1, part)


def other_columns(rows, lines, target_count, panel, *refs):
    pieces, refs = refs[:lines], refs[lines:]
    pp, tp, pm_old, tm_old, norms, total, coded, pm, tm, *weights = refs
    ring, height, width = panel.shape
    pm[...] = pm_old[...]
    tm[...] = tm_old[...]
    kernels_into(panel, norms, pieces, weights, (pm, tm), rows)
    weight = total[:1, :1]
    for at in range(0, ring * height, rows):
        part = slice(at, at + rows)
        pool_pull = pp[part, :] + pulled(weights, pieces, 0, part)
        target_pull = tp[part, :] + pulled(weights, pieces, 1, part)
        pool_mass = jnp.sum(pm[part, :], axis=1, keepdims=True)
        target_mass = jnp.sum(tm[part, :], axis=1, keepdims=True)
        own = panel[at // height : (at + rows) // height].reshape(rows, width).astype(F32)
        proof = target_mass / target_count - pool_mass / weight
        term = (target_pull - target_mass * own) * (1.0 / target_count) - (
            pool_pull - pool_mass * own
        ) * (1.0 / weight)
        code = encode(term, proof)
        for i in range(rows // height):
            coded[at // height + i] = code[i * height : (i + 1) * height, :]


def step_scale(step):
    return jnp.exp2(step * (1.0 / 128.0))


def encode(term, proof):
    top = jnp.maximum(jnp.max(jnp.abs(term), axis=1, keepdims=True), 1e-30)
    step = jnp.ceil(jnp.log2(top) * 128.0)
    steps = jnp.round(term * (LEVELS / step_scale(step)))
    steps = jnp.clip(steps, -LEVELS, LEVELS)
    first = jnp.round(proof * 8192.0)
    rest = (proof * 8192.0 - first) * 32768.0
    second = jnp.round(rest)
    third = jnp.round((rest - second) * 32768.0)
    lane = lax.broadcasted_iota(jnp.int32, (term.shape[0], LANES), 1)
    notes = jnp.where(
        lane == 0, step, jnp.where(lane == 1, first, jnp.where(lane == 2, second, third))
    )
    return jnp.concatenate([steps, notes], axis=1).astype(jnp.int32).astype(jnp.int16)


def add_terms(coded, proof, gradient):
    width = gradient.shape[1]
    total, small = 0.0, 0.0
    for i in range(coded.shape[0]):
        code = coded[i].astype(jnp.int32).astype(F32)
        notes = code[:, width:]
        total += code[:, :width] * (step_scale(notes[:, :1]) * (1.0 / LEVELS))
        parts = notes[:, 1:2], notes[:, 2:3], notes[:, 3:4]
        small += (parts[0] + (parts[1] + parts[2] * (1.0 / 32768.0)) * (1.0 / 32768.0)) * (1.0 / 8192.0)
    gradient[...] = total
    proof[...] = along_lanes(small)


def place(z):
    return z % 2 * 4 + z // 2


def handed_on(arrays, awaited):
    spec = pl.BlockSpec(memory_space=pl.ANY)
    return pl.pallas_call(
        lambda *refs: None,
        out_shape=[shape(a.shape, a.dtype) for a in arrays],
        in_specs=[spec] * (len(arrays) + 1),
        out_specs=[spec] * len(arrays),
        input_output_aliases={i: i for i in range(len(arrays))},
        name="handed_on",
    )(*arrays, awaited)


def along_line(x, shift, phase):
    pairs = []
    for i in range(4):
        for j in range(4):
            for c in range(2):
                there = (shift(i), j) if (c + phase) % 2 == 0 else (i, shift(j))
                pairs.append(((i * 2 + c) * 4 + j, (there[0] * 2 + c) * 4 + there[1]))
    return lax.ppermute(x, PLANE, pairs)


def line(x, phase):
    return [x] + [along_line(x, lambda i, k=k: (i + k) % 4, phase) for k in (1, 3, 2)]


def other_core(x):
    return lax.ppermute(x, "c", [(0, 1), (1, 0)])


def on_device(pool, targets, counts):
    ring = lax.axis_size(RING)
    height, width = pool.shape
    rows = ring * height
    target_count = float(height * lax.axis_size(AXES))

    block, copies = in_vmem(
        pack_block,
        "pack_block",
        (shape((2 * height + META, width), BF16), shape((ring, height, width), BF16)),
    )(pool, targets, counts.reshape(1, height))
    blocks = line(block, 0)
    panel = lax.all_to_all(copies, RING, split_axis=0, concat_axis=0, tiled=True)
    piece, total = in_vmem(
        pack_line,
        "pack_line",
        (shape((2 * height * len(blocks) + META, width), BF16), shape((8, LANES), F32)),
    )(*blocks)
    pieces = line(piece, 1)
    for bit in (1, 2):
        total = total + along_line(total, lambda i: i ^ bit, 1)
    for bit in (1, 2, 4):
        total = total + lax.ppermute(total, RING, [(place(i), place(i ^ bit)) for i in range(ring)])
    total = total + other_core(total)
    pieces = [piece, *handed_on(pieces[1:], total)]
    others = [other_core(p) for p in pieces]

    columns = height * len(blocks) * len(pieces)
    flops = 8 * rows * columns * width
    weights = [pltpu.VMEM((rows, columns), BF16)] * 2
    state = in_vmem(
        functools.partial(own_columns, 256, len(pieces)),
        "own_columns",
        (shape((rows, width), F32),) * 2 + (shape((rows, LANES), F32),) * 3,
        flops=flops,
        scratch=weights,
        limit=28,
    )(panel, *pieces)
    coded = in_vmem(
        functools.partial(other_columns, 256, len(pieces), target_count),
        "other_columns",
        shape((ring, height, width + LANES), jnp.int16),
        flops=flops,
        scratch=[pltpu.VMEM((rows, LANES), F32)] * 2 + weights,
        limit=28,
    )(panel, *others, *state, total)
    coded = lax.all_to_all(coded, RING, split_axis=0, concat_axis=0, tiled=True)
    proof, gradient = in_vmem(
        add_terms, "add_terms", (shape((1, height), F32), shape((height, width), F32))
    )(coded)
    return proof.reshape(height), gradient


def solution(mesh):
    split = Mesh(mesh.devices.reshape(2, 4, 2, 4, 4), AXES)
    return jax.shard_map(
        on_device,
        mesh=split,
        in_specs=(P(AXES, None), P(AXES, None), P(AXES)),
        out_specs=(P(AXES), P(AXES, None)),
        check_vma=False,
    )
```

```python
import functools

import jax
import jax.numpy as jnp
from jax import lax
from jax.experimental import pallas as pl
from jax.experimental.pallas import tpu as pltpu
from jax.sharding import Mesh
from jax.sharding import PartitionSpec as P

AXES = ("zl", "x", "c", "y", "zh")
RING = ("zl", "zh")
PLANE = ("x", "c", "y")
LANES = 128
META = 16
LEVELS = 32767.0
OFFSETS = (3, 1, 5, 7, 4, 2, 6, 0)
F32, BF16 = jnp.float32, jnp.bfloat16


def shape(dims, dtype):
    return jax.ShapeDtypeStruct(dims, dtype)


def in_vmem(body, name, out_shape, flops=0, traffic=1 << 20, scratch=(), limit=16, aliases=None):
    spec = pl.BlockSpec(memory_space=pltpu.VMEM)

    def call(*args):
        return pl.pallas_call(
            body,
            out_shape=out_shape,
            in_specs=[spec] * len(args),
            out_specs=jax.tree.map(lambda _: spec, out_shape),
            scratch_shapes=scratch,
            compiler_params=pltpu.CompilerParams(vmem_limit_bytes=limit << 20),
            cost_estimate=pl.CostEstimate(flops=flops, bytes_accessed=traffic, transcendentals=0),
            input_output_aliases=aliases or {},
            name=name,
        )(*args)

    return call


def lane_sums(x):
    total = x[:, :LANES]
    for at in range(LANES, x.shape[1], LANES):
        total = total + x[:, at : at + LANES]
    return total


def square_norms(block):
    wide = block.astype(F32)
    return jnp.sum(lane_sums(wide * wide), axis=1, keepdims=True)


def along_lanes(column):
    return jnp.transpose(jnp.broadcast_to(column, (column.shape[0], LANES)))[:1]


def halves(a, b):
    return jnp.concatenate([a, b], axis=1)


def pack_block(pool, targets, counts, block, copies):
    height = pool.shape[0]
    block[:height, :] = pool[...]
    block[height : 2 * height, :] = targets[...]
    norms = along_lanes(jnp.concatenate([square_norms(pool[...]), square_norms(targets[...])], axis=0))
    high = norms.astype(BF16).astype(F32)
    middle = (norms - high).astype(BF16).astype(F32)
    low = norms - high - middle
    weights = halves(counts[...].astype(F32), jnp.ones((1, height), F32))
    meta = jnp.concatenate([weights, high, middle, low, jnp.zeros((META - 4, LANES), F32)], axis=0)
    block[2 * height :, :] = jnp.concatenate(
        [meta, jnp.zeros((META, block.shape[1] - LANES), F32)], axis=1
    ).astype(BF16)
    for i in range(copies.shape[0]):
        copies[i] = pool[...]


def pack_line(*refs):
    blocks, piece = refs[:-1], refs[-1]
    count, height = len(blocks), (blocks[0].shape[0] - META) // 2
    for j, block in enumerate(blocks):
        piece[j * height : (j + 1) * height, :] = block[:height, :]
        piece[(count + j) * height : (count + j + 1) * height, :] = block[height : 2 * height, :]
    metas = [block[2 * height :, :LANES].astype(F32) for block in blocks]
    lanes = [meta[:, half : half + height] for half in (0, height) for meta in metas]
    pairs = [halves(a, b) for a, b in zip(lanes[::2], lanes[1::2])]
    width = piece.shape[1] - LANES * len(pairs)
    piece[2 * count * height :, :] = jnp.concatenate(
        [*pairs, jnp.zeros((META, width), F32)], axis=1
    ).astype(BF16)


def add_columns(panel, norms, pieces, pulls, masses, weights, rows, first):
    height, width = panel.shape
    size = (pieces[0].shape[0] - META) // 2
    for half in range(2):
        for i, piece in enumerate(pieces):
            columns = piece[half * size : (half + 1) * size, :]
            meta = piece[2 * size :, half * size : (half + 1) * size].astype(F32)
            col_norms = meta[1:2] + meta[2:3] + meta[3:4]
            for at in range(0, height, rows):
                part = slice(at, at + rows)
                inner = lax.dot_general(
                    panel[part, :], columns, (((1,), (1,)), ((), ())), preferred_element_type=F32
                )
                squared = norms[part, :1] + col_norms - 2.0 * inner
                kernel = jnp.exp(-squared * (0.5 / width))
                if half == 0:
                    kernel = kernel * meta[:1]
                if first and i == 0:
                    masses[half][part, :] = lane_sums(kernel)
                else:
                    masses[half][part, :] += lane_sums(kernel)
                weights[half][part, i * size : (i + 1) * size] = kernel.astype(BF16)
    for half in range(2):
        for at in range(0, height, rows):
            part = slice(at, at + rows)
            total = None if first else pulls[half][part, :]
            for i, piece in enumerate(pieces):
                one = jnp.dot(
                    weights[half][part, i * size : (i + 1) * size],
                    piece[half * size : (half + 1) * size, :],
                    preferred_element_type=F32,
                )
                total = one if total is None else total + one
            pulls[half][part, :] = total


def first_columns(rows, lines, panel, *refs):
    pieces, refs = refs[:lines], refs[lines:]
    ordered, norms, pp, tp, pm, tm, *weights = refs
    ring, height, _ = panel.shape
    z = 2 * lax.axis_index("zh") + lax.axis_index("zl")
    for i, offset in enumerate(OFFSETS):
        part = slice(i * height, (i + 1) * height)
        there = lax.rem(z + offset, ring)
        block = panel[lax.rem(there, 2) * 4 + lax.div(there, 2)]
        ordered[part, :] = block
        norms[part, :] = jnp.broadcast_to(square_norms(block), (height, LANES))
    add_columns(ordered, norms, pieces, (pp, tp), (pm, tm), weights, rows, True)


def more_columns(rows, lines, panel, norms, *refs):
    pieces, refs = refs[:lines], refs[lines + 4 :]
    pp, tp, pm, tm, *weights = refs
    add_columns(panel, norms, pieces, (pp, tp), (pm, tm), weights, rows, False)


def count_chosen(*refs):
    pieces, chosen = refs[:-1], refs[-1]
    size = (pieces[0].shape[0] - META) // 2
    total = jnp.zeros((1, size), F32)
    for piece in pieces:
        total = total + piece[2 * size :, :size].astype(F32)[:1]
    chosen[...] = jnp.full(chosen.shape, jnp.sum(total), F32)


def terms(target_count, panel, pp, tp, pm, tm, total, part):
    weight = total[:1, :1]
    pool_mass = jnp.sum(pm[part, :], axis=1, keepdims=True)
    target_mass = jnp.sum(tm[part, :], axis=1, keepdims=True)
    own = panel[part, :].astype(F32)
    proof = target_mass / target_count - pool_mass / weight
    gradient = (tp[part, :] - target_mass * own) * (1.0 / target_count) - (
        pp[part, :] - pool_mass * own
    ) * (1.0 / weight)
    return gradient, proof


def far_terms(target_count, height, *refs):
    inputs, (up, down, up_half, down_half) = refs[:6], refs[6:]
    for i in range(4):
        code = encode(*terms(target_count, *inputs, slice(i * height, (i + 1) * height)))
        (up, down)[i // 2][i % 2 * height : (i % 2 + 1) * height, :] = code
    code = encode(*terms(target_count, *inputs, slice(4 * height, 5 * height)))
    down_half[...] = code[: height // 2, :]
    up_half[...] = code[height // 2 :, :]


def near_terms(target_count, height, *refs):
    inputs, (gradient, proof) = refs[:6], refs[6:]
    for i in range(5, 8):
        part = slice((i - 5) * height, (i - 4) * height)
        gradient[part, :], small = terms(target_count, *inputs, slice(i * height, (i + 1) * height))
        proof[part, :] = jnp.broadcast_to(small, (height, LANES))


def pass_on(gradient, proof, from_below, from_above, half_below, half_above, up, down):
    width, height = gradient.shape[1], gradient.shape[0] // 3
    for i, near, half, out in ((0, from_below, half_below, up), (1, from_above, half_above, down)):
        part = slice(i * height, (i + 1) * height)
        near_gradient, near_proof = decode(near[:height, :], width)
        half_gradient, half_proof = decode(half[...], width)
        zeros = jnp.zeros((height // 2, width), F32), jnp.zeros((height // 2, 1), F32)
        both = [(half_gradient, zeros[0]), (half_proof, zeros[1])]
        if i == 0:
            both = [pair[::-1] for pair in both]
        half_gradient, half_proof = (jnp.concatenate(pair, axis=0) for pair in both)
        out[...] = encode(
            gradient[part, :] + near_gradient + half_gradient,
            proof[part, :1] + near_proof + half_proof,
        )


def add_up(gradient, proof, from_below, from_above, far_below, far_above, out_proof, out):
    width, height = gradient.shape[1], gradient.shape[0] // 3
    total, small = gradient[2 * height :, :], proof[2 * height :, :1]
    for coded in (from_below[height:, :], from_above[height:, :], far_below[...], far_above[...]):
        one, part = decode(coded, width)
        total, small = total + one, small + part
    out[...] = total
    out_proof[...] = along_lanes(small)


def step_scale(step):
    return jnp.exp2(step * (1.0 / 128.0))


def encode(term, proof):
    top = jnp.maximum(jnp.max(jnp.abs(term), axis=1, keepdims=True), 1e-30)
    step = jnp.ceil(jnp.log2(top) * 128.0)
    steps = jnp.round(term * (LEVELS / step_scale(step)))
    steps = jnp.clip(steps, -LEVELS, LEVELS)
    first = jnp.round(proof * 8192.0)
    rest = (proof * 8192.0 - first) * 32768.0
    second = jnp.round(rest)
    third = jnp.round((rest - second) * 32768.0)
    lane = lax.broadcasted_iota(jnp.int32, (term.shape[0], LANES), 1)
    notes = jnp.where(
        lane == 0, step, jnp.where(lane == 1, first, jnp.where(lane == 2, second, third))
    )
    return jnp.concatenate([steps, notes], axis=1).astype(jnp.int32).astype(jnp.int16)


def decode(coded, width):
    code = coded.astype(jnp.int32).astype(F32)
    notes = code[:, width:]
    first, second, third = notes[:, 1:2], notes[:, 2:3], notes[:, 3:4]
    proof = (first + (second + third * (1.0 / 32768.0)) * (1.0 / 32768.0)) * (1.0 / 8192.0)
    return code[:, :width] * (step_scale(notes[:, :1]) * (1.0 / LEVELS)), proof


def place(z):
    return z % 2 * 4 + z // 2


def up_the_ring(x, step):
    ring = lax.axis_size(RING)
    return lax.ppermute(x, RING, [(place(i), place((i + step) % ring)) for i in range(ring)])


def along_line(x, shift, phase):
    pairs = []
    for i in range(4):
        for j in range(4):
            for c in range(2):
                there = (shift(i), j) if (c + phase) % 2 == 0 else (i, shift(j))
                pairs.append(((i * 2 + c) * 4 + j, (there[0] * 2 + c) * 4 + there[1]))
    return lax.ppermute(x, PLANE, pairs)


def line(x, phase):
    return [x] + [along_line(x, lambda i, k=k: (i + k) % 4, phase) for k in (1, 3, 2)]


def other_core(x):
    return lax.ppermute(x, "c", [(0, 1), (1, 0)])


def on_device(pool, targets, counts):
    ring = lax.axis_size(RING)
    height, width = pool.shape
    rows = ring * height
    target_count = float(height * lax.axis_size(AXES))

    block, copies = in_vmem(
        pack_block,
        "pack_block",
        (shape((2 * height + META, width), BF16), shape((ring, height, width), BF16)),
        limit=56,
    )(pool, targets, counts.reshape(1, height))
    blocks = line(block, 0)
    panel = lax.all_to_all(copies, RING, split_axis=0, concat_axis=0, tiled=True)
    piece = in_vmem(
        pack_line, "pack_line", shape((2 * height * len(blocks) + META, width), BF16)
    )(*blocks)
    pieces = line(piece, 1)
    others = [other_core(p) for p in pieces]

    size = height * len(blocks)
    sums = (shape((rows, width), F32),) * 2 + (shape((rows, LANES), F32),) * 2

    def add(body, arrays, some, state, out_shape, aliases):
        return in_vmem(
            functools.partial(body, 256, len(some)),
            body.__name__,
            out_shape,
            flops=8 * rows * len(some) * size * width,
            scratch=[pltpu.VMEM((rows, len(some) * size), BF16)] * 2,
            limit=20,
            aliases=aliases,
        )(*arrays, *some, *state)

    def more(some, state):
        return add(more_columns, (panel, norms), some, state, sums, {2 + len(some) + i: i for i in range(4)})

    panel, norms, *state = add(
        first_columns,
        (panel,),
        (pieces[0], others[0]),
        (),
        (shape((rows, width), BF16), shape((rows, LANES), F32), *sums),
        {},
    )
    state = more(pieces[1:3], state)
    total = in_vmem(count_chosen, "count_chosen", shape((8, LANES), F32))(*pieces, *others)
    for bit in (1, 2, 4):
        total = total + lax.ppermute(total, RING, [(place(i), place(i ^ bit)) for i in range(ring)])
    for some in ((pieces[3], others[1]), others[2:3], others[3:]):
        state = more(some, state)

    inputs = panel, *state, total
    whole, half = (shape((n, width + LANES), jnp.int16) for n in (2 * height, height // 2))
    up, down, up_half, down_half = in_vmem(
        functools.partial(far_terms, target_count, height),
        "far_terms",
        (whole, whole, half, half),
    )(*inputs)
    from_above, from_below = up_the_ring(down, ring - 1), up_the_ring(up, 1)
    half_above, half_below = up_the_ring(down_half, ring - 2), up_the_ring(up_half, 2)
    near = in_vmem(
        functools.partial(near_terms, target_count, height),
        "near_terms",
        (shape((3 * height, width), F32), shape((3 * height, LANES), F32)),
    )(*inputs)
    up, down = in_vmem(pass_on, "pass_on", (shape((height, width + LANES), jnp.int16),) * 2)(
        *near, from_below, from_above, half_below, half_above
    )
    far_above, far_below = up_the_ring(down, ring - 2), up_the_ring(up, 2)
    proof, gradient = in_vmem(
        add_up, "add_up", (shape((1, height), F32), shape((height, width), F32))
    )(*near, from_below, from_above, far_below, far_above)
    return proof.reshape(height), gradient


def solution(mesh):
    split = Mesh(mesh.devices.reshape(2, 4, 2, 4, 4), AXES)
    return jax.shard_map(
        on_device,
        mesh=split,
        in_specs=(P(AXES, None), P(AXES, None), P(AXES)),
        out_specs=(P(AXES), P(AXES, None)),
        check_vma=False,
    )
```

```python
import functools

import jax
import jax.numpy as jnp
from jax import lax
from jax.experimental import pallas as pl
from jax.experimental.pallas import tpu as pltpu
from jax.sharding import Mesh
from jax.sharding import PartitionSpec as P

AXES = ("zl", "x", "c", "y", "zh")
RING = ("zl", "zh")
PLANE = ("x", "c", "y")
LANES = 128
META = 16
LEVELS = 32767.0
OFFSETS = (3, 1, 5, 7, 4, 2, 6, 0)
F32, BF16 = jnp.float32, jnp.bfloat16


def shape(dims, dtype):
    return jax.ShapeDtypeStruct(dims, dtype)


def in_vmem(body, name, out_shape, flops=0, traffic=1 << 20, scratch=(), limit=12, aliases=None):
    spec = pl.BlockSpec(memory_space=pltpu.VMEM)

    def call(*args):
        return pl.pallas_call(
            body,
            out_shape=out_shape,
            in_specs=[spec] * len(args),
            out_specs=jax.tree.map(lambda _: spec, out_shape),
            scratch_shapes=scratch,
            compiler_params=pltpu.CompilerParams(vmem_limit_bytes=limit << 20),
            cost_estimate=pl.CostEstimate(flops=flops, bytes_accessed=traffic, transcendentals=0),
            input_output_aliases=aliases or {},
            name=name,
        )(*args)

    return call


def lane_sums(x):
    total = x[:, :LANES]
    for at in range(LANES, x.shape[1], LANES):
        total = total + x[:, at : at + LANES]
    return total


def square_norms(block):
    wide = block.astype(F32)
    return jnp.sum(lane_sums(wide * wide), axis=1, keepdims=True)


def along_lanes(column):
    return jnp.transpose(jnp.broadcast_to(column, (column.shape[0], LANES)))[:1]


def halves(a, b):
    return jnp.concatenate([a, b], axis=1)


def pack_block(pool, targets, counts, block):
    height = pool.shape[0]
    block[:height, :] = pool[...]
    block[height : 2 * height, :] = targets[...]
    norms = along_lanes(jnp.concatenate([square_norms(pool[...]), square_norms(targets[...])], axis=0))
    high = norms.astype(BF16).astype(F32)
    middle = (norms - high).astype(BF16).astype(F32)
    low = norms - high - middle
    weights = halves(counts[...].astype(F32), jnp.ones((1, height), F32))
    meta = jnp.concatenate([weights, high, middle, low, jnp.zeros((META - 4, LANES), F32)], axis=0)
    block[2 * height :, :] = jnp.concatenate(
        [meta, jnp.zeros((META, block.shape[1] - LANES), F32)], axis=1
    ).astype(BF16)


def pack_line(*refs):
    blocks, (own, below, above, opposite, piece, up_pair, down_pair, across) = refs[:-8], refs[-8:]
    across[...] = opposite[...]
    up_pair[...] = jnp.concatenate([own[...], below[...]], axis=0)
    down_pair[...] = jnp.concatenate([own[...], above[...]], axis=0)
    count, height = len(blocks), (blocks[0].shape[0] - META) // 2
    for j, block in enumerate(blocks):
        piece[j * height : (j + 1) * height, :] = block[:height, :]
        piece[(count + j) * height : (count + j + 1) * height, :] = block[height : 2 * height, :]
    metas = [block[2 * height :, :LANES].astype(F32) for block in blocks]
    lanes = [meta[:, half : half + height] for half in (0, height) for meta in metas]
    pairs = [halves(a, b) for a, b in zip(lanes[::2], lanes[1::2])]
    width = piece.shape[1] - LANES * len(pairs)
    piece[2 * count * height :, :] = jnp.concatenate(
        [*pairs, jnp.zeros((META, width), F32)], axis=1
    ).astype(BF16)


def add_columns(panel, norms, pieces, old, pulls, masses, weights, rows):
    height, width = panel.shape
    size = (pieces[0].shape[0] - META) // 2
    for half in range(2):
        for i, piece in enumerate(pieces):
            columns = piece[half * size : (half + 1) * size, :]
            meta = piece[2 * size :, half * size : (half + 1) * size].astype(F32)
            col_norms = meta[1:2] + meta[2:3] + meta[3:4]
            for at in range(0, height, rows):
                part = slice(at, at + rows)
                inner = lax.dot_general(
                    panel[part, :], columns, (((1,), (1,)), ((), ())), preferred_element_type=F32
                )
                squared = norms[part, :1] + col_norms - 2.0 * inner
                kernel = jnp.exp(-squared * (0.5 / width))
                if half == 0:
                    kernel = kernel * meta[:1]
                mass = lane_sums(kernel)
                if i > 0:
                    mass = masses[half][part, :] + mass
                elif old:
                    mass = old[2 + half][part, :] + mass
                masses[half][part, :] = mass
                weights[half][part, i * size : (i + 1) * size] = kernel.astype(BF16)
    for half in range(2):
        for at in range(0, height, rows):
            part = slice(at, at + rows)
            total = old[half][part, :] if old else None
            for i, piece in enumerate(pieces):
                one = jnp.dot(
                    weights[half][part, i * size : (i + 1) * size],
                    piece[half * size : (half + 1) * size, :],
                    preferred_element_type=F32,
                )
                total = one if total is None else total + one
            pulls[half][part, :] = total


def first_columns(rows, lines, own, below, above, opposite, pair_below, pair_above, *refs):
    pieces, refs = refs[:lines], refs[lines:]
    ordered, norms, pp, tp, pm, tm, *weights = refs
    height = own.shape[0]
    found = {0: own, 1: above, 7: below, 4: opposite}
    for i, offset in enumerate(OFFSETS):
        part = slice(i * height, (i + 1) * height)
        if offset in found:
            block = found[offset][...]
        else:
            pair, at = (pair_above, offset - 2) if offset < 4 else (pair_below, 6 - offset)
            block = pair[at * height : (at + 1) * height, :]
        ordered[part, :] = block
        norms[part, :] = jnp.broadcast_to(square_norms(block), (height, LANES))
    add_columns(ordered, norms, pieces, (), (pp, tp), (pm, tm), weights, rows)


def more_columns(rows, lines, panel, norms, *refs):
    pieces, old, refs = refs[:lines], refs[lines : lines + 4], refs[lines + 4 :]
    pp, tp, pm, tm, *weights = refs
    add_columns(panel, norms, pieces, old, (pp, tp), (pm, tm), weights, rows)


def count_chosen(*refs):
    metas, chosen = refs[:-1], refs[-1]
    total = sum(meta[...].astype(F32)[:1] for meta in metas)
    chosen[...] = jnp.full(chosen.shape, jnp.sum(total), F32)


def terms(target_count, panel, pp, tp, pm, tm, total, part):
    weight = total[:1, :1]
    pool_mass = jnp.sum(pm[part, :], axis=1, keepdims=True)
    target_mass = jnp.sum(tm[part, :], axis=1, keepdims=True)
    own = panel[part, :].astype(F32)
    proof = target_mass / target_count - pool_mass / weight
    gradient = (tp[part, :] - target_mass * own) * (1.0 / target_count) - (
        pp[part, :] - pool_mass * own
    ) * (1.0 / weight)
    return gradient, proof


def far_terms(target_count, height, *refs):
    inputs, (up, down, up_half, down_half) = refs[:6], refs[6:]
    for i in range(4):
        code = encode(*terms(target_count, *inputs, slice(i * height, (i + 1) * height)))
        (up, down)[i // 2][i % 2 * height : (i % 2 + 1) * height, :] = code
    code = encode(*terms(target_count, *inputs, slice(4 * height, 5 * height)))
    down_half[...] = code[: height // 2, :]
    up_half[...] = code[height // 2 :, :]


def near_terms(target_count, height, *refs):
    inputs, (gradient, proof) = refs[:6], refs[6:]
    for i in range(5, 8):
        part = slice((i - 5) * height, (i - 4) * height)
        gradient[part, :], small = terms(target_count, *inputs, slice(i * height, (i + 1) * height))
        proof[part, :] = jnp.broadcast_to(small, (height, LANES))


def pass_on(gradient, proof, from_below, from_above, half_below, half_above, up, down):
    width, height = gradient.shape[1], gradient.shape[0] // 3
    for i, near, half, out in ((0, from_below, half_below, up), (1, from_above, half_above, down)):
        part = slice(i * height, (i + 1) * height)
        near_gradient, near_proof = decode(near[:height, :], width)
        half_gradient, half_proof = decode(half[...], width)
        zeros = jnp.zeros((height // 2, width), F32), jnp.zeros((height // 2, 1), F32)
        both = [(half_gradient, zeros[0]), (half_proof, zeros[1])]
        if i == 0:
            both = [pair[::-1] for pair in both]
        half_gradient, half_proof = (jnp.concatenate(pair, axis=0) for pair in both)
        out[...] = encode(
            gradient[part, :] + near_gradient + half_gradient,
            proof[part, :1] + near_proof + half_proof,
        )


def add_up(gradient, proof, from_below, from_above, far_below, far_above, out_proof, out):
    width, height = gradient.shape[1], gradient.shape[0] // 3
    total, small = gradient[2 * height :, :], proof[2 * height :, :1]
    for coded in (from_below[height:, :], from_above[height:, :], far_below[...], far_above[...]):
        one, part = decode(coded, width)
        total, small = total + one, small + part
    out[...] = total
    out_proof[...] = along_lanes(small)


def step_scale(step):
    return jnp.exp2(step * (1.0 / 128.0))


def encode(term, proof):
    top = jnp.maximum(jnp.max(jnp.abs(term), axis=1, keepdims=True), 1e-30)
    step = jnp.ceil(jnp.log2(top) * 128.0)
    steps = jnp.round(term * (LEVELS / step_scale(step)))
    steps = jnp.clip(steps, -LEVELS, LEVELS)
    first = jnp.round(proof * 8192.0)
    rest = (proof * 8192.0 - first) * 32768.0
    second = jnp.round(rest)
    third = jnp.round((rest - second) * 32768.0)
    lane = lax.broadcasted_iota(jnp.int32, (term.shape[0], LANES), 1)
    notes = jnp.where(
        lane == 0, step, jnp.where(lane == 1, first, jnp.where(lane == 2, second, third))
    )
    return jnp.concatenate([steps, notes], axis=1).astype(jnp.int32).astype(jnp.int16)


def decode(coded, width):
    code = coded.astype(jnp.int32).astype(F32)
    notes = code[:, width:]
    first, second, third = notes[:, 1:2], notes[:, 2:3], notes[:, 3:4]
    proof = (first + (second + third * (1.0 / 32768.0)) * (1.0 / 32768.0)) * (1.0 / 8192.0)
    return code[:, :width] * (step_scale(notes[:, :1]) * (1.0 / LEVELS)), proof


def place(z):
    return z % 2 * 4 + z // 2


def handed_on(array, awaited):
    there = pl.BlockSpec(memory_space=pl.ANY)
    return pl.pallas_call(
        lambda *refs: None,
        out_shape=shape(array.shape, array.dtype),
        in_specs=[there, pl.BlockSpec(memory_space=pltpu.VMEM)],
        out_specs=there,
        input_output_aliases={0: 0},
        compiler_params=pltpu.CompilerParams(vmem_limit_bytes=4 << 20),
        name="handed_on",
    )(array, awaited)


def up_the_ring(x, step):
    ring = lax.axis_size(RING)
    return lax.ppermute(x, RING, [(place(i), place((i + step) % ring)) for i in range(ring)])


def along_line(x, shift, phase):
    pairs = []
    for i in range(4):
        for j in range(4):
            for c in range(2):
                there = (shift(i), j) if (c + phase) % 2 == 0 else (i, shift(j))
                pairs.append(((i * 2 + c) * 4 + j, (there[0] * 2 + c) * 4 + there[1]))
    return lax.ppermute(x, PLANE, pairs)


def line(x, phase):
    return [x] + [along_line(x, lambda i, k=k: (i + k) % 4, phase) for k in (1, 3, 2)]


def other_core(x):
    return lax.ppermute(x, "c", [(0, 1), (1, 0)])


def on_device(pool, targets, counts):
    ring = lax.axis_size(RING)
    height, width = pool.shape
    rows = ring * height
    target_count = float(height * lax.axis_size(AXES))

    block = in_vmem(pack_block, "pack_block", shape((2 * height + META, width), BF16), limit=56)(
        pool, targets, counts.reshape(1, height)
    )
    blocks = line(block, 0)
    below, above, opposite = (up_the_ring(pool, step) for step in (1, ring - 1, ring // 2))
    pair = shape((2 * height, width), BF16)
    piece, up_pair, down_pair, opposite = in_vmem(
        pack_line,
        "pack_line",
        (shape((2 * height * len(blocks) + META, width), BF16), pair, pair, shape(pool.shape, BF16)),
    )(*blocks, pool, below, above, opposite)
    pieces = line(piece, 1)
    pairs = up_the_ring(up_pair, 2), up_the_ring(down_pair, ring - 2)
    others = [other_core(p) for p in pieces[:3]]

    size = height * len(blocks)
    sums = (shape((rows, width), F32),) * 2 + (shape((rows, LANES), F32),) * 2

    def add(body, arrays, some, state, out_shape, aliases):
        return in_vmem(
            functools.partial(body, 256, len(some)),
            body.__name__,
            out_shape,
            flops=8 * rows * len(some) * size * width,
            scratch=[pltpu.VMEM((rows, len(some) * size), BF16)] * 2,
            limit=12,
            aliases=aliases,
        )(*arrays, *some, *state)

    def more(some, state):
        return add(more_columns, (panel, norms), some, state, sums, {2 + len(some) + i: i for i in range(4)})

    panel, norms, *state = add(
        first_columns,
        (pool, below, above, opposite, *pairs),
        pieces[:1],
        (),
        (shape((rows, width), BF16), shape((rows, LANES), F32), *sums),
        {},
    )
    state = more(pieces[1:3], state)
    pieces[3] = handed_on(pieces[3], state[2])
    others.append(other_core(pieces[3]))
    total = pl.pallas_call(
        count_chosen,
        grid=(1,),
        out_shape=shape((8, LANES), F32),
        in_specs=[pl.BlockSpec((META, size), lambda i: (2 * size // META, 0))] * 2 * len(pieces),
        out_specs=pl.BlockSpec((8, LANES), lambda i: (0, 0)),
        name="count_chosen",
        compiler_params=pltpu.CompilerParams(vmem_limit_bytes=4 << 20),
    )(*pieces, *others)
    for bit in (1, 2, 4):
        total = total + lax.ppermute(total, RING, [(place(i), place(i ^ bit)) for i in range(ring)])
    for some in (pieces[3:], others[:2], others[2:3], others[3:]):
        state = more(some, state)

    inputs = panel, *state, total
    whole, half = (shape((n, width + LANES), jnp.int16) for n in (2 * height, height // 2))
    up, down, up_half, down_half = in_vmem(
        functools.partial(far_terms, target_count, height),
        "far_terms",
        (whole, whole, half, half),
    )(*inputs)
    from_above, from_below = up_the_ring(down, ring - 1), up_the_ring(up, 1)
    half_above, half_below = up_the_ring(down_half, ring - 2), up_the_ring(up_half, 2)
    near = in_vmem(
        functools.partial(near_terms, target_count, height),
        "near_terms",
        (shape((3 * height, width), F32), shape((3 * height, LANES), F32)),
    )(*inputs)
    up, down = in_vmem(pass_on, "pass_on", (shape((height, width + LANES), jnp.int16),) * 2)(
        *near, from_below, from_above, half_below, half_above
    )
    far_above, far_below = up_the_ring(down, ring - 2), up_the_ring(up, 2)
    proof, gradient = in_vmem(
        add_up, "add_up", (shape((1, height), F32), shape((height, width), F32))
    )(*near, from_below, from_above, far_below, far_above)
    return proof.reshape(height), gradient


def solution(mesh):
    split = Mesh(mesh.devices.reshape(2, 4, 2, 4, 4), AXES)
    return jax.shard_map(
        on_device,
        mesh=split,
        in_specs=(P(AXES, None), P(AXES, None), P(AXES)),
        out_specs=(P(AXES), P(AXES, None)),
        check_vma=False,
    )
```

```python
import functools

import jax
import jax.numpy as jnp
from jax import lax
from jax.experimental import pallas as pl
from jax.experimental.pallas import tpu as pltpu
from jax.sharding import Mesh
from jax.sharding import PartitionSpec as P

AXES = ("zl", "x", "c", "y", "zh")
RING = ("zl", "zh")
PLANE = ("x", "c", "y")
LANES = 128
META = 16
LEVELS = 32767.0
OFFSETS = (3, 1, 5, 7, 4, 2, 6, 0)
F32, BF16 = jnp.float32, jnp.bfloat16


def shape(dims, dtype):
    return jax.ShapeDtypeStruct(dims, dtype)


def in_vmem(body, name, out_shape, flops=0, traffic=1 << 20, scratch=(), limit=12, aliases=None):
    spec = pl.BlockSpec(memory_space=pltpu.VMEM)

    def call(*args):
        return pl.pallas_call(
            body,
            out_shape=out_shape,
            in_specs=[spec] * len(args),
            out_specs=jax.tree.map(lambda _: spec, out_shape),
            scratch_shapes=scratch,
            compiler_params=pltpu.CompilerParams(vmem_limit_bytes=limit << 20),
            cost_estimate=pl.CostEstimate(flops=flops, bytes_accessed=traffic, transcendentals=0),
            input_output_aliases=aliases or {},
            name=name,
        )(*args)

    return call


def lane_sums(x):
    total = x[:, :LANES]
    for at in range(LANES, x.shape[1], LANES):
        total = total + x[:, at : at + LANES]
    return total


def square_norms(block):
    wide = block.astype(F32)
    return jnp.sum(lane_sums(wide * wide), axis=1, keepdims=True)


def along_lanes(column):
    return jnp.transpose(jnp.broadcast_to(column, (column.shape[0], LANES)))[:1]


def halves(a, b):
    return jnp.concatenate([a, b], axis=1)


def pack_block(pool, targets, counts, block):
    height = pool.shape[0]
    block[:height, :] = pool[...]
    block[height : 2 * height, :] = targets[...]
    norms = along_lanes(jnp.concatenate([square_norms(pool[...]), square_norms(targets[...])], axis=0))
    high = norms.astype(BF16).astype(F32)
    middle = (norms - high).astype(BF16).astype(F32)
    low = norms - high - middle
    weights = halves(counts[...].astype(F32), jnp.ones((1, height), F32))
    meta = jnp.concatenate([weights, high, middle, low, jnp.zeros((META - 4, LANES), F32)], axis=0)
    block[2 * height :, :] = jnp.concatenate(
        [meta, jnp.zeros((META, block.shape[1] - LANES), F32)], axis=1
    ).astype(BF16)


def pack_line(*refs):
    blocks, (own, below, above, piece, up_pair, down_pair) = refs[:-6], refs[-6:]
    half = own.shape[0] // 2
    up_pair[...] = jnp.concatenate([own[...], above[...], below[:half, :]], axis=0)
    down_pair[...] = jnp.concatenate([own[...], below[...], above[half:, :]], axis=0)
    count, height = len(blocks), (blocks[0].shape[0] - META) // 2
    for j, block in enumerate(blocks):
        piece[j * height : (j + 1) * height, :] = block[:height, :]
        piece[(count + j) * height : (count + j + 1) * height, :] = block[height : 2 * height, :]
    metas = [block[2 * height :, :LANES].astype(F32) for block in blocks]
    lanes = [meta[:, half : half + height] for half in (0, height) for meta in metas]
    pairs = [halves(a, b) for a, b in zip(lanes[::2], lanes[1::2])]
    width = piece.shape[1] - LANES * len(pairs)
    piece[2 * count * height :, :] = jnp.concatenate(
        [*pairs, jnp.zeros((META, width), F32)], axis=1
    ).astype(BF16)


def add_columns(panel, norms, pieces, old, pulls, masses, weights, rows):
    height, width = panel.shape
    size = (pieces[0].shape[0] - META) // 2
    for half in range(2):
        for i, piece in enumerate(pieces):
            columns = piece[half * size : (half + 1) * size, :]
            meta = piece[2 * size :, half * size : (half + 1) * size].astype(F32)
            col_norms = meta[1:2] + meta[2:3] + meta[3:4]
            for at in range(0, height, rows):
                part = slice(at, at + rows)
                inner = lax.dot_general(
                    panel[part, :], columns, (((1,), (1,)), ((), ())), preferred_element_type=F32
                )
                squared = norms[part, :1] + col_norms - 2.0 * inner
                kernel = jnp.exp(-squared * (0.5 / width))
                if half == 0:
                    kernel = kernel * meta[:1]
                mass = lane_sums(kernel)
                if i > 0:
                    mass = masses[half][part, :] + mass
                elif old:
                    mass = old[2 + half][part, :] + mass
                masses[half][part, :] = mass
                weights[half][part, i * size : (i + 1) * size] = kernel.astype(BF16)
    for half in range(2):
        for at in range(0, height, rows):
            part = slice(at, at + rows)
            total = old[half][part, :] if old else None
            for i, piece in enumerate(pieces):
                one = jnp.dot(
                    weights[half][part, i * size : (i + 1) * size],
                    piece[half * size : (half + 1) * size, :],
                    preferred_element_type=F32,
                )
                total = one if total is None else total + one
            pulls[half][part, :] = total


def first_columns(rows, lines, own, below, above, far_below, far_above, *refs):
    pieces, refs = refs[:lines], refs[lines:]
    ordered, norms, pp, tp, pm, tm, *weights = refs
    height = own.shape[0]
    found = {
        0: own[...],
        1: above[...],
        7: below[...],
        3: far_above[:height, :],
        2: far_above[height : 2 * height, :],
        5: far_below[:height, :],
        6: far_below[height : 2 * height, :],
        4: jnp.concatenate([far_below[2 * height :, :], far_above[2 * height :, :]], axis=0),
    }
    for i, offset in enumerate(OFFSETS):
        part = slice(i * height, (i + 1) * height)
        block = found[offset]
        ordered[part, :] = block
        norms[part, :] = jnp.broadcast_to(square_norms(block), (height, LANES))
    add_columns(ordered, norms, pieces, (), (pp, tp), (pm, tm), weights, rows)


def more_columns(rows, lines, panel, norms, *refs):
    pieces, old, refs = refs[:lines], refs[lines : lines + 4], refs[lines + 4 :]
    pp, tp, pm, tm, *weights = refs
    add_columns(panel, norms, pieces, old, (pp, tp), (pm, tm), weights, rows)


def count_chosen(*refs):
    metas, chosen = refs[:-1], refs[-1]
    total = sum(meta[...].astype(F32)[:1] for meta in metas)
    chosen[...] = jnp.full(chosen.shape, jnp.sum(total), F32)


def terms(target_count, panel, pp, tp, pm, tm, total, part):
    weight = total[:1, :1]
    pool_mass = jnp.sum(pm[part, :], axis=1, keepdims=True)
    target_mass = jnp.sum(tm[part, :], axis=1, keepdims=True)
    own = panel[part, :].astype(F32)
    proof = target_mass / target_count - pool_mass / weight
    gradient = (tp[part, :] - target_mass * own) * (1.0 / target_count) - (
        pp[part, :] - pool_mass * own
    ) * (1.0 / weight)
    return gradient, proof


def far_terms(target_count, height, *refs):
    inputs, (up, down, up_half, down_half) = refs[:6], refs[6:]
    for i in range(4):
        code = encode(*terms(target_count, *inputs, slice(i * height, (i + 1) * height)))
        (up, down)[i // 2][i % 2 * height : (i % 2 + 1) * height, :] = code
    code = encode(*terms(target_count, *inputs, slice(4 * height, 5 * height)))
    down_half[...] = code[: height // 2, :]
    up_half[...] = code[height // 2 :, :]


def near_terms(target_count, height, *refs):
    inputs, (gradient, proof) = refs[:6], refs[6:]
    for i in range(5, 8):
        part = slice((i - 5) * height, (i - 4) * height)
        gradient[part, :], small = terms(target_count, *inputs, slice(i * height, (i + 1) * height))
        proof[part, :] = jnp.broadcast_to(small, (height, LANES))


def pass_on(gradient, proof, from_below, from_above, half_below, half_above, up, down):
    width, height = gradient.shape[1], gradient.shape[0] // 3
    for i, near, half, out in ((0, from_below, half_below, up), (1, from_above, half_above, down)):
        part = slice(i * height, (i + 1) * height)
        near_gradient, near_proof = decode(near[:height, :], width)
        half_gradient, half_proof = decode(half[...], width)
        zeros = jnp.zeros((height // 2, width), F32), jnp.zeros((height // 2, 1), F32)
        both = [(half_gradient, zeros[0]), (half_proof, zeros[1])]
        if i == 0:
            both = [pair[::-1] for pair in both]
        half_gradient, half_proof = (jnp.concatenate(pair, axis=0) for pair in both)
        out[...] = encode(
            gradient[part, :] + near_gradient + half_gradient,
            proof[part, :1] + near_proof + half_proof,
        )


def add_up(gradient, proof, from_below, from_above, far_below, far_above, out_proof, out):
    width, height = gradient.shape[1], gradient.shape[0] // 3
    total, small = gradient[2 * height :, :], proof[2 * height :, :1]
    for coded in (from_below[height:, :], from_above[height:, :], far_below[...], far_above[...]):
        one, part = decode(coded, width)
        total, small = total + one, small + part
    out[...] = total
    out_proof[...] = along_lanes(small)


def step_scale(step):
    return jnp.exp2(step * (1.0 / 128.0))


def encode(term, proof):
    top = jnp.maximum(jnp.max(jnp.abs(term), axis=1, keepdims=True), 1e-30)
    step = jnp.ceil(jnp.log2(top) * 128.0)
    steps = jnp.round(term * (LEVELS / step_scale(step)))
    steps = jnp.clip(steps, -LEVELS, LEVELS)
    first = jnp.round(proof * 8192.0)
    rest = (proof * 8192.0 - first) * 32768.0
    second = jnp.round(rest)
    third = jnp.round((rest - second) * 32768.0)
    lane = lax.broadcasted_iota(jnp.int32, (term.shape[0], LANES), 1)
    notes = jnp.where(
        lane == 0, step, jnp.where(lane == 1, first, jnp.where(lane == 2, second, third))
    )
    return jnp.concatenate([steps, notes], axis=1).astype(jnp.int32).astype(jnp.int16)


def decode(coded, width):
    code = coded.astype(jnp.int32).astype(F32)
    notes = code[:, width:]
    first, second, third = notes[:, 1:2], notes[:, 2:3], notes[:, 3:4]
    proof = (first + (second + third * (1.0 / 32768.0)) * (1.0 / 32768.0)) * (1.0 / 8192.0)
    return code[:, :width] * (step_scale(notes[:, :1]) * (1.0 / LEVELS)), proof


def place(z):
    return z % 2 * 4 + z // 2


def handed_on(arrays, *awaited):
    there = pl.BlockSpec(memory_space=pl.ANY)
    return pl.pallas_call(
        lambda *refs: None,
        out_shape=[shape(a.shape, a.dtype) for a in arrays],
        in_specs=[there] * (len(arrays) + len(awaited)),
        out_specs=[there] * len(arrays),
        input_output_aliases={i: i for i in range(len(arrays))},
        compiler_params=pltpu.CompilerParams(vmem_limit_bytes=4 << 20),
        name="handed_on",
    )(*arrays, *awaited)


def up_the_ring(x, step):
    ring = lax.axis_size(RING)
    return lax.ppermute(x, RING, [(place(i), place((i + step) % ring)) for i in range(ring)])


def along_line(x, shift, phase):
    pairs = []
    for i in range(4):
        for j in range(4):
            for c in range(2):
                there = (shift(i), j) if (c + phase) % 2 == 0 else (i, shift(j))
                pairs.append(((i * 2 + c) * 4 + j, (there[0] * 2 + c) * 4 + there[1]))
    return lax.ppermute(x, PLANE, pairs)


def line(x, phase):
    return [x] + [along_line(x, lambda i, k=k: (i + k) % 4, phase) for k in (1, 3, 2)]


def other_core(x):
    return lax.ppermute(x, "c", [(0, 1), (1, 0)])


def on_device(pool, targets, counts):
    ring = lax.axis_size(RING)
    height, width = pool.shape
    rows = ring * height
    target_count = float(height * lax.axis_size(AXES))

    block = in_vmem(pack_block, "pack_block", shape((2 * height + META, width), BF16), limit=56)(
        pool, targets, counts.reshape(1, height)
    )
    blocks = line(block, 0)
    below, above = up_the_ring(pool, 1), up_the_ring(pool, ring - 1)
    pair = shape((5 * height // 2, width), BF16)
    piece, up_pair, down_pair = in_vmem(
        pack_line, "pack_line", (shape((2 * height * len(blocks) + META, width), BF16), pair, pair)
    )(*blocks, pool, below, above)
    pieces = line(piece, 1)
    pairs = up_the_ring(up_pair, 3), up_the_ring(down_pair, ring - 3)
    others = [other_core(piece)]

    size = height * len(blocks)
    sums = (shape((rows, width), F32),) * 2 + (shape((rows, LANES), F32),) * 2

    def add(body, arrays, some, state, out_shape, aliases):
        return in_vmem(
            functools.partial(body, 256, len(some)),
            body.__name__,
            out_shape,
            flops=8 * rows * len(some) * size * width,
            scratch=[pltpu.VMEM((rows, len(some) * size), BF16)] * 2,
            limit=12,
            aliases=aliases,
        )(*arrays, *some, *state)

    def more(some, state):
        return add(more_columns, (panel, norms), some, state, sums, {2 + len(some) + i: i for i in range(4)})

    panel, norms, *state = add(
        first_columns,
        (pool, below, above, *pairs),
        pieces[:1],
        (),
        (shape((rows, width), BF16), shape((rows, LANES), F32), *sums),
        {},
    )
    pieces[1:3] = handed_on(pieces[1:3], norms)
    others += [other_core(p) for p in pieces[1:3]]
    state = more(pieces[1:3], state)
    pieces[3:] = handed_on(pieces[3:], state[2], *others[1:3])
    others.append(other_core(pieces[3]))
    total = pl.pallas_call(
        count_chosen,
        grid=(1,),
        out_shape=shape((8, LANES), F32),
        in_specs=[pl.BlockSpec((META, size), lambda i: (2 * size // META, 0))] * 2 * len(pieces),
        out_specs=pl.BlockSpec((8, LANES), lambda i: (0, 0)),
        name="count_chosen",
        compiler_params=pltpu.CompilerParams(vmem_limit_bytes=4 << 20),
    )(*pieces, *others)
    for bit in (1, 2, 4):
        total = total + lax.ppermute(total, RING, [(place(i), place(i ^ bit)) for i in range(ring)])
    for some in (pieces[3:], others[:2], others[2:3], others[3:]):
        state = more(some, state)

    inputs = panel, *state, total
    whole, half = (shape((n, width + LANES), jnp.int16) for n in (2 * height, height // 2))
    up, down, up_half, down_half = in_vmem(
        functools.partial(far_terms, target_count, height),
        "far_terms",
        (whole, whole, half, half),
    )(*inputs)
    from_above, from_below = up_the_ring(down, ring - 1), up_the_ring(up, 1)
    half_above, half_below = up_the_ring(down_half, ring - 2), up_the_ring(up_half, 2)
    near = in_vmem(
        functools.partial(near_terms, target_count, height),
        "near_terms",
        (shape((3 * height, width), F32), shape((3 * height, LANES), F32)),
    )(*inputs)
    up, down = in_vmem(pass_on, "pass_on", (shape((height, width + LANES), jnp.int16),) * 2)(
        *near, from_below, from_above, half_below, half_above
    )
    far_above, far_below = up_the_ring(down, ring - 2), up_the_ring(up, 2)
    proof, gradient = in_vmem(
        add_up, "add_up", (shape((1, height), F32), shape((height, width), F32))
    )(*near, from_below, from_above, far_below, far_above)
    return proof.reshape(height), gradient


def solution(mesh):
    split = Mesh(mesh.devices.reshape(2, 4, 2, 4, 4), AXES)
    return jax.shard_map(
        on_device,
        mesh=split,
        in_specs=(P(AXES, None), P(AXES, None), P(AXES)),
        out_specs=(P(AXES), P(AXES, None)),
        check_vma=False,
    )
```

```python
import functools

import jax
import jax.numpy as jnp
from jax import lax
from jax.experimental import pallas as pl
from jax.experimental.pallas import tpu as pltpu
from jax.sharding import Mesh
from jax.sharding import PartitionSpec as P

AXES = ("zl", "x", "c", "y", "zh")
RING = ("zl", "zh")
PLANE = ("x", "c", "y")
LANES = 128
META = 16
LEVELS = 32767.0
OFFSETS = (3, 1, 5, 7, 4, 2, 6, 0)
F32, BF16 = jnp.float32, jnp.bfloat16


def shape(dims, dtype):
    return jax.ShapeDtypeStruct(dims, dtype)


def in_vmem(body, name, out_shape, flops=0, traffic=1 << 20, scratch=(), limit=12, aliases=None):
    spec = pl.BlockSpec(memory_space=pltpu.VMEM)

    def call(*args):
        return pl.pallas_call(
            body,
            out_shape=out_shape,
            in_specs=[spec] * len(args),
            out_specs=jax.tree.map(lambda _: spec, out_shape),
            scratch_shapes=scratch,
            compiler_params=pltpu.CompilerParams(vmem_limit_bytes=limit << 20),
            cost_estimate=pl.CostEstimate(flops=flops, bytes_accessed=traffic, transcendentals=0),
            input_output_aliases=aliases or {},
            name=name,
        )(*args)

    return call


def lane_sums(x):
    total = x[:, :LANES]
    for at in range(LANES, x.shape[1], LANES):
        total = total + x[:, at : at + LANES]
    return total


def square_norms(block):
    wide = block.astype(F32)
    return jnp.sum(lane_sums(wide * wide), axis=1, keepdims=True)


def along_lanes(column):
    return jnp.transpose(jnp.broadcast_to(column, (column.shape[0], LANES)))[:1]


def halves(a, b):
    return jnp.concatenate([a, b], axis=1)


def pack_block(pool, targets, counts, block):
    height = pool.shape[0]
    block[:height, :] = pool[...]
    block[height : 2 * height, :] = targets[...]
    norms = along_lanes(jnp.concatenate([square_norms(pool[...]), square_norms(targets[...])], axis=0))
    high = norms.astype(BF16).astype(F32)
    middle = (norms - high).astype(BF16).astype(F32)
    low = norms - high - middle
    weights = halves(counts[...].astype(F32), jnp.ones((1, height), F32))
    meta = jnp.concatenate([weights, high, middle, low, jnp.zeros((META - 4, LANES), F32)], axis=0)
    block[2 * height :, :] = jnp.concatenate(
        [meta, jnp.zeros((META, block.shape[1] - LANES), F32)], axis=1
    ).astype(BF16)


def pack_line(*refs):
    blocks, (own, below, above, piece, up_pair, down_pair) = refs[:-6], refs[-6:]
    half = own.shape[0] // 2
    up_pair[...] = jnp.concatenate([own[...], above[...], below[:half, :]], axis=0)
    down_pair[...] = jnp.concatenate([own[...], below[...], above[half:, :]], axis=0)
    count, height = len(blocks), (blocks[0].shape[0] - META) // 2
    for j, block in enumerate(blocks):
        piece[j * height : (j + 1) * height, :] = block[:height, :]
        piece[(count + j) * height : (count + j + 1) * height, :] = block[height : 2 * height, :]
    metas = [block[2 * height :, :LANES].astype(F32) for block in blocks]
    lanes = [meta[:, half : half + height] for half in (0, height) for meta in metas]
    pairs = [halves(a, b) for a, b in zip(lanes[::2], lanes[1::2])]
    width = piece.shape[1] - LANES * len(pairs)
    piece[2 * count * height :, :] = jnp.concatenate(
        [*pairs, jnp.zeros((META, width), F32)], axis=1
    ).astype(BF16)


def add_columns(panel, norms, pieces, old, pulls, masses, weights, rows):
    height, width = panel.shape
    size = (pieces[0].shape[0] - META) // 2
    for half in range(2):
        for i, piece in enumerate(pieces):
            columns = piece[half * size : (half + 1) * size, :]
            meta = piece[2 * size :, half * size : (half + 1) * size].astype(F32)
            col_norms = meta[1:2] + meta[2:3] + meta[3:4]
            for at in range(0, height, rows):
                part = slice(at, at + rows)
                inner = lax.dot_general(
                    panel[part, :], columns, (((1,), (1,)), ((), ())), preferred_element_type=F32
                )
                squared = norms[part, :1] + col_norms - 2.0 * inner
                kernel = jnp.exp(-squared * (0.5 / width))
                if half == 0:
                    kernel = kernel * meta[:1]
                mass = lane_sums(kernel)
                if i > 0:
                    mass = masses[half][part, :] + mass
                elif old:
                    mass = old[2 + half][part, :] + mass
                masses[half][part, :] = mass
                weights[half][part, i * size : (i + 1) * size] = kernel.astype(BF16)
    for half in range(2):
        for at in range(0, height, rows):
            part = slice(at, at + rows)
            total = old[half][part, :] if old else None
            for i, piece in enumerate(pieces):
                one = jnp.dot(
                    weights[half][part, i * size : (i + 1) * size],
                    piece[half * size : (half + 1) * size, :],
                    preferred_element_type=F32,
                )
                total = one if total is None else total + one
            pulls[half][part, :] = total


def first_columns(rows, lines, own, below, above, far_below, far_above, chosen, *refs):
    pieces, refs = refs[:lines], refs[lines:]
    ordered, norms, total, pp, tp, pm, tm, *weights = refs
    total[...] = jnp.broadcast_to(jnp.sum(chosen[...], axis=0), total.shape)
    height = own.shape[0]
    found = {
        0: own[...],
        1: above[...],
        7: below[...],
        3: far_above[:height, :],
        2: far_above[height : 2 * height, :],
        5: far_below[:height, :],
        6: far_below[height : 2 * height, :],
        4: jnp.concatenate([far_below[2 * height :, :], far_above[2 * height :, :]], axis=0),
    }
    for i, offset in enumerate(OFFSETS):
        part = slice(i * height, (i + 1) * height)
        block = found[offset]
        ordered[part, :] = block
        norms[part, :] = jnp.broadcast_to(square_norms(block), (height, LANES))
    add_columns(ordered, norms, pieces, (), (pp, tp), (pm, tm), weights, rows)


def more_columns(rows, lines, panel, norms, *refs):
    pieces, old, refs = refs[:lines], refs[lines : lines + 4], refs[lines + 4 :]
    pp, tp, pm, tm, *weights = refs
    add_columns(panel, norms, pieces, old, (pp, tp), (pm, tm), weights, rows)


def terms(target_count, panel, pp, tp, pm, tm, total, part):
    weight = total[:1, :1]
    pool_mass = jnp.sum(pm[part, :], axis=1, keepdims=True)
    target_mass = jnp.sum(tm[part, :], axis=1, keepdims=True)
    own = panel[part, :].astype(F32)
    proof = target_mass / target_count - pool_mass / weight
    gradient = (tp[part, :] - target_mass * own) * (1.0 / target_count) - (
        pp[part, :] - pool_mass * own
    ) * (1.0 / weight)
    return gradient, proof


def far_terms(target_count, height, *refs):
    inputs, (up, down, up_half, down_half) = refs[:6], refs[6:]
    for i in range(4):
        code = encode(*terms(target_count, *inputs, slice(i * height, (i + 1) * height)))
        (up, down)[i // 2][i % 2 * height : (i % 2 + 1) * height, :] = code
    code = encode(*terms(target_count, *inputs, slice(4 * height, 5 * height)))
    down_half[...] = code[: height // 2, :]
    up_half[...] = code[height // 2 :, :]


def near_terms(target_count, height, *refs):
    inputs, (gradient, proof) = refs[:6], refs[6:]
    for i in range(5, 8):
        part = slice((i - 5) * height, (i - 4) * height)
        gradient[part, :], small = terms(target_count, *inputs, slice(i * height, (i + 1) * height))
        proof[part, :] = jnp.broadcast_to(small, (height, LANES))


def pass_on(gradient, proof, from_below, from_above, half_below, half_above, up, down):
    width, height = gradient.shape[1], gradient.shape[0] // 3
    for i, near, half, out in ((0, from_below, half_below, up), (1, from_above, half_above, down)):
        part = slice(i * height, (i + 1) * height)
        near_gradient, near_proof = decode(near[:height, :], width)
        half_gradient, half_proof = decode(half[...], width)
        zeros = jnp.zeros((height // 2, width), F32), jnp.zeros((height // 2, 1), F32)
        both = [(half_gradient, zeros[0]), (half_proof, zeros[1])]
        if i == 0:
            both = [pair[::-1] for pair in both]
        half_gradient, half_proof = (jnp.concatenate(pair, axis=0) for pair in both)
        out[...] = encode(
            gradient[part, :] + near_gradient + half_gradient,
            proof[part, :1] + near_proof + half_proof,
        )


def add_up(gradient, proof, from_below, from_above, far_below, far_above, out_proof, out):
    width, height = gradient.shape[1], gradient.shape[0] // 3
    total, small = gradient[2 * height :, :], proof[2 * height :, :1]
    for coded in (from_below[height:, :], from_above[height:, :], far_below[...], far_above[...]):
        one, part = decode(coded, width)
        total, small = total + one, small + part
    out[...] = total
    out_proof[...] = along_lanes(small)


def step_scale(step):
    return jnp.exp2(step * (1.0 / 128.0))


def encode(term, proof):
    top = jnp.maximum(jnp.max(jnp.abs(term), axis=1, keepdims=True), 1e-30)
    step = jnp.ceil(jnp.log2(top) * 128.0)
    steps = jnp.round(term * (LEVELS / step_scale(step)))
    steps = jnp.clip(steps, -LEVELS, LEVELS)
    first = jnp.round(proof * 8192.0)
    rest = (proof * 8192.0 - first) * 32768.0
    second = jnp.round(rest)
    third = jnp.round((rest - second) * 32768.0)
    lane = lax.broadcasted_iota(jnp.int32, (term.shape[0], LANES), 1)
    notes = jnp.where(
        lane == 0, step, jnp.where(lane == 1, first, jnp.where(lane == 2, second, third))
    )
    return jnp.concatenate([steps, notes], axis=1).astype(jnp.int32).astype(jnp.int16)


def decode(coded, width):
    code = coded.astype(jnp.int32).astype(F32)
    notes = code[:, width:]
    first, second, third = notes[:, 1:2], notes[:, 2:3], notes[:, 3:4]
    proof = (first + (second + third * (1.0 / 32768.0)) * (1.0 / 32768.0)) * (1.0 / 8192.0)
    return code[:, :width] * (step_scale(notes[:, :1]) * (1.0 / LEVELS)), proof


def place(z):
    return z % 2 * 4 + z // 2


def handed_on(arrays, *awaited):
    there = pl.BlockSpec(memory_space=pl.ANY)
    return pl.pallas_call(
        lambda *refs: None,
        out_shape=[shape(a.shape, a.dtype) for a in arrays],
        in_specs=[there] * (len(arrays) + len(awaited)),
        out_specs=[there] * len(arrays),
        input_output_aliases={i: i for i in range(len(arrays))},
        compiler_params=pltpu.CompilerParams(vmem_limit_bytes=4 << 20),
        name="handed_on",
    )(*arrays, *awaited)


def up_the_ring(x, step):
    ring = lax.axis_size(RING)
    return lax.ppermute(x, RING, [(place(i), place((i + step) % ring)) for i in range(ring)])


def along_line(x, shift, phase):
    pairs = []
    for i in range(4):
        for j in range(4):
            for c in range(2):
                there = (shift(i), j) if (c + phase) % 2 == 0 else (i, shift(j))
                pairs.append(((i * 2 + c) * 4 + j, (there[0] * 2 + c) * 4 + there[1]))
    return lax.ppermute(x, PLANE, pairs)


def line(x, phase):
    return [x] + [along_line(x, lambda i, k=k: (i + k) % 4, phase) for k in (1, 3, 2)]


def other_core(x):
    return lax.ppermute(x, "c", [(0, 1), (1, 0)])


def on_device(pool, targets, counts):
    ring = lax.axis_size(RING)
    height, width = pool.shape
    rows = ring * height
    target_count = float(height * lax.axis_size(AXES))

    devices = lax.axis_size(AXES)
    chosen = jnp.broadcast_to(jnp.sum(counts).astype(F32), (devices, 1, LANES))
    chosen = lax.all_to_all(chosen, AXES, split_axis=0, concat_axis=0, tiled=True)
    block = in_vmem(pack_block, "pack_block", shape((2 * height + META, width), BF16), limit=56)(
        pool, targets, counts.reshape(1, height)
    )
    blocks = line(block, 0)
    below, above = up_the_ring(pool, 1), up_the_ring(pool, ring - 1)
    pair = shape((5 * height // 2, width), BF16)
    piece, up_pair, down_pair = in_vmem(
        pack_line, "pack_line", (shape((2 * height * len(blocks) + META, width), BF16), pair, pair)
    )(*blocks, pool, below, above)
    pieces = line(piece, 1)
    pairs = up_the_ring(up_pair, 3), up_the_ring(down_pair, ring - 3)
    others = [other_core(piece)]

    size = height * len(blocks)
    sums = (shape((rows, width), F32),) * 2 + (shape((rows, LANES), F32),) * 2

    def add(body, arrays, some, state, out_shape, aliases):
        return in_vmem(
            functools.partial(body, 256, len(some)),
            body.__name__,
            out_shape,
            flops=8 * rows * len(some) * size * width,
            scratch=[pltpu.VMEM((rows, len(some) * size), BF16)] * 2,
            limit=12,
            aliases=aliases,
        )(*arrays, *some, *state)

    def more(some, state):
        return add(more_columns, (panel, norms), some, state, sums, {2 + len(some) + i: i for i in range(4)})

    panel, norms, total, *state = add(
        first_columns,
        (pool, below, above, *pairs, chosen),
        pieces[:1],
        (),
        (shape((rows, width), BF16), shape((rows, LANES), F32), shape((8, LANES), F32), *sums),
        {},
    )
    pieces[1:] = handed_on(pieces[1:], norms)
    others += [other_core(p) for p in pieces[1:]]
    for some in (pieces[1:3], (pieces[3], others[0]), others[1:]):
        state = more(some, state)

    inputs = panel, *state, total
    whole, half = (shape((n, width + LANES), jnp.int16) for n in (2 * height, height // 2))
    up, down, up_half, down_half = in_vmem(
        functools.partial(far_terms, target_count, height),
        "far_terms",
        (whole, whole, half, half),
    )(*inputs)
    from_above, from_below = up_the_ring(down, ring - 1), up_the_ring(up, 1)
    half_above, half_below = up_the_ring(down_half, ring - 2), up_the_ring(up_half, 2)
    near = in_vmem(
        functools.partial(near_terms, target_count, height),
        "near_terms",
        (shape((3 * height, width), F32), shape((3 * height, LANES), F32)),
    )(*inputs)
    up, down = in_vmem(pass_on, "pass_on", (shape((height, width + LANES), jnp.int16),) * 2)(
        *near, from_below, from_above, half_below, half_above
    )
    far_above, far_below = up_the_ring(down, ring - 2), up_the_ring(up, 2)
    proof, gradient = in_vmem(
        add_up, "add_up", (shape((1, height), F32), shape((height, width), F32))
    )(*near, from_below, from_above, far_below, far_above)
    return proof.reshape(height), gradient


def solution(mesh):
    split = Mesh(mesh.devices.reshape(2, 4, 2, 4, 4), AXES)
    return jax.shard_map(
        on_device,
        mesh=split,
        in_specs=(P(AXES, None), P(AXES, None), P(AXES)),
        out_specs=(P(AXES), P(AXES, None)),
        check_vma=False,
    )
```

```python
import functools

import jax
import jax.numpy as jnp
from jax import lax
from jax.experimental import pallas as pl
from jax.experimental.pallas import tpu as pltpu
from jax.sharding import Mesh
from jax.sharding import PartitionSpec as P

AXES = ("zl", "x", "c", "y", "zh")
RING = ("zl", "zh")
CHIPS = ("zl", "x", "y", "zh")
PLANE = ("x", "c", "y")
LANES = 128
META = 16
LEVELS = 32767.0
OFFSETS = (3, 1, 5, 7, 4, 2, 6, 0)
F32, BF16 = jnp.float32, jnp.bfloat16


def shape(dims, dtype):
    return jax.ShapeDtypeStruct(dims, dtype)


def in_vmem(body, name, out_shape, flops=0, traffic=1 << 20, scratch=(), limit=12, aliases=None):
    spec = pl.BlockSpec(memory_space=pltpu.VMEM)

    def call(*args):
        return pl.pallas_call(
            body,
            out_shape=out_shape,
            in_specs=[spec] * len(args),
            out_specs=jax.tree.map(lambda _: spec, out_shape),
            scratch_shapes=scratch,
            compiler_params=pltpu.CompilerParams(vmem_limit_bytes=limit << 20),
            cost_estimate=pl.CostEstimate(flops=flops, bytes_accessed=traffic, transcendentals=0),
            input_output_aliases=aliases or {},
            name=name,
        )(*args)

    return call


def lane_sums(x):
    total = x[:, :LANES]
    for at in range(LANES, x.shape[1], LANES):
        total = total + x[:, at : at + LANES]
    return total


def square_norms(block):
    wide = block.astype(F32)
    return jnp.sum(lane_sums(wide * wide), axis=1, keepdims=True)


def along_lanes(column):
    return jnp.transpose(jnp.broadcast_to(column, (column.shape[0], LANES)))[:1]


def halves(a, b):
    return jnp.concatenate([a, b], axis=1)


def pack_block(pool, targets, counts, block, chosen):
    height = pool.shape[0]
    chosen[...] = jnp.full(chosen.shape, jnp.sum(counts[...].astype(F32)), F32)
    block[:height, :] = pool[...]
    block[height : 2 * height, :] = targets[...]
    norms = along_lanes(jnp.concatenate([square_norms(pool[...]), square_norms(targets[...])], axis=0))
    high = norms.astype(BF16).astype(F32)
    middle = (norms - high).astype(BF16).astype(F32)
    low = norms - high - middle
    weights = halves(counts[...].astype(F32), jnp.ones((1, height), F32))
    meta = jnp.concatenate([weights, high, middle, low, jnp.zeros((META - 4, LANES), F32)], axis=0)
    block[2 * height :, :] = jnp.concatenate(
        [meta, jnp.zeros((META, block.shape[1] - LANES), F32)], axis=1
    ).astype(BF16)


def pack_line(*refs):
    blocks, (own, below, above, piece, up_pair, down_pair) = refs[:-6], refs[-6:]
    half = own.shape[0] // 2
    up_pair[...] = jnp.concatenate([own[...], above[...], below[:half, :]], axis=0)
    down_pair[...] = jnp.concatenate([own[...], below[...], above[half:, :]], axis=0)
    count, height = len(blocks), (blocks[0].shape[0] - META) // 2
    for j, block in enumerate(blocks):
        piece[j * height : (j + 1) * height, :] = block[:height, :]
        piece[(count + j) * height : (count + j + 1) * height, :] = block[height : 2 * height, :]
    metas = [block[2 * height :, :LANES].astype(F32) for block in blocks]
    lanes = [meta[:, half : half + height] for half in (0, height) for meta in metas]
    pairs = [halves(a, b) for a, b in zip(lanes[::2], lanes[1::2])]
    width = piece.shape[1] - LANES * len(pairs)
    piece[2 * count * height :, :] = jnp.concatenate(
        [*pairs, jnp.zeros((META, width), F32)], axis=1
    ).astype(BF16)


def add_columns(panel, norms, pieces, old, pulls, masses, weights, rows):
    height, width = panel.shape
    size = (pieces[0].shape[0] - META) // 2
    for half in range(2):
        for i, piece in enumerate(pieces):
            columns = piece[half * size : (half + 1) * size, :]
            meta = piece[2 * size :, half * size : (half + 1) * size].astype(F32)
            col_norms = meta[1:2] + meta[2:3] + meta[3:4]
            for at in range(0, height, rows):
                part = slice(at, at + rows)
                inner = lax.dot_general(
                    panel[part, :], columns, (((1,), (1,)), ((), ())), preferred_element_type=F32
                )
                squared = norms[part, :1] + col_norms - 2.0 * inner
                kernel = jnp.exp(-squared * (0.5 / width))
                if half == 0:
                    kernel = kernel * meta[:1]
                mass = lane_sums(kernel)
                if i > 0:
                    mass = masses[half][part, :] + mass
                elif old:
                    mass = old[2 + half][part, :] + mass
                masses[half][part, :] = mass
                weights[half][part, i * size : (i + 1) * size] = kernel.astype(BF16)
    for half in range(2):
        for at in range(0, height, rows):
            part = slice(at, at + rows)
            total = old[half][part, :] if old else None
            for i, piece in enumerate(pieces):
                one = jnp.dot(
                    weights[half][part, i * size : (i + 1) * size],
                    piece[half * size : (half + 1) * size, :],
                    preferred_element_type=F32,
                )
                total = one if total is None else total + one
            pulls[half][part, :] = total


def first_columns(rows, lines, own, below, above, far_below, far_above, chosen, *refs):
    pieces, refs = refs[:lines], refs[lines:]
    ordered, norms, total, pp, tp, pm, tm, *weights = refs
    total[...] = jnp.broadcast_to(jnp.sum(chosen[...], axis=0), total.shape)
    height = own.shape[0]
    found = {
        0: own[...],
        1: above[...],
        7: below[...],
        3: far_above[:height, :],
        2: far_above[height : 2 * height, :],
        5: far_below[:height, :],
        6: far_below[height : 2 * height, :],
        4: jnp.concatenate([far_below[2 * height :, :], far_above[2 * height :, :]], axis=0),
    }
    for i, offset in enumerate(OFFSETS):
        part = slice(i * height, (i + 1) * height)
        block = found[offset]
        ordered[part, :] = block
        norms[part, :] = jnp.broadcast_to(square_norms(block), (height, LANES))
    add_columns(ordered, norms, pieces, (), (pp, tp), (pm, tm), weights, rows)


def more_columns(rows, lines, panel, norms, *refs):
    pieces, old, refs = refs[:lines], refs[lines : lines + 4], refs[lines + 4 :]
    pp, tp, pm, tm, *weights = refs
    add_columns(panel, norms, pieces, old, (pp, tp), (pm, tm), weights, rows)


def terms(target_count, panel, pp, tp, pm, tm, total, other_total, part):
    weight = total[:1, :1] + other_total[:1, :1]
    pool_mass = jnp.sum(pm[part, :], axis=1, keepdims=True)
    target_mass = jnp.sum(tm[part, :], axis=1, keepdims=True)
    own = panel[part, :].astype(F32)
    proof = target_mass / target_count - pool_mass / weight
    gradient = (tp[part, :] - target_mass * own) * (1.0 / target_count) - (
        pp[part, :] - pool_mass * own
    ) * (1.0 / weight)
    return gradient, proof


def far_terms(target_count, height, *refs):
    inputs, (up, down, up_half, down_half) = refs[:7], refs[7:]
    for i in range(4):
        code = encode(*terms(target_count, *inputs, slice(i * height, (i + 1) * height)))
        (up, down)[i // 2][i % 2 * height : (i % 2 + 1) * height, :] = code
    code = encode(*terms(target_count, *inputs, slice(4 * height, 5 * height)))
    down_half[...] = code[: height // 2, :]
    up_half[...] = code[height // 2 :, :]


def near_terms(target_count, height, *refs):
    inputs, (gradient, proof) = refs[:7], refs[7:]
    for i in range(5, 8):
        part = slice((i - 5) * height, (i - 4) * height)
        gradient[part, :], small = terms(target_count, *inputs, slice(i * height, (i + 1) * height))
        proof[part, :] = jnp.broadcast_to(small, (height, LANES))


def pass_on(gradient, proof, from_below, from_above, half_below, half_above, up, down):
    width, height = gradient.shape[1], gradient.shape[0] // 3
    for i, near, half, out in ((0, from_below, half_below, up), (1, from_above, half_above, down)):
        part = slice(i * height, (i + 1) * height)
        near_gradient, near_proof = decode(near[:height, :], width)
        half_gradient, half_proof = decode(half[...], width)
        zeros = jnp.zeros((height // 2, width), F32), jnp.zeros((height // 2, 1), F32)
        both = [(half_gradient, zeros[0]), (half_proof, zeros[1])]
        if i == 0:
            both = [pair[::-1] for pair in both]
        half_gradient, half_proof = (jnp.concatenate(pair, axis=0) for pair in both)
        out[...] = encode(
            gradient[part, :] + near_gradient + half_gradient,
            proof[part, :1] + near_proof + half_proof,
        )


def add_up(gradient, proof, from_below, from_above, far_below, far_above, out_proof, out):
    width, height = gradient.shape[1], gradient.shape[0] // 3
    total, small = gradient[2 * height :, :], proof[2 * height :, :1]
    for coded in (from_below[height:, :], from_above[height:, :], far_below[...], far_above[...]):
        one, part = decode(coded, width)
        total, small = total + one, small + part
    out[...] = total
    out_proof[...] = along_lanes(small)


def step_scale(step):
    return jnp.exp2(step * (1.0 / 128.0))


def encode(term, proof):
    top = jnp.maximum(jnp.max(jnp.abs(term), axis=1, keepdims=True), 1e-30)
    step = jnp.ceil(jnp.log2(top) * 128.0)
    steps = jnp.round(term * (LEVELS / step_scale(step)))
    steps = jnp.clip(steps, -LEVELS, LEVELS)
    first = jnp.round(proof * 8192.0)
    rest = (proof * 8192.0 - first) * 32768.0
    second = jnp.round(rest)
    third = jnp.round((rest - second) * 32768.0)
    lane = lax.broadcasted_iota(jnp.int32, (term.shape[0], LANES), 1)
    notes = jnp.where(
        lane == 0, step, jnp.where(lane == 1, first, jnp.where(lane == 2, second, third))
    )
    return jnp.concatenate([steps, notes], axis=1).astype(jnp.int32).astype(jnp.int16)


def decode(coded, width):
    code = coded.astype(jnp.int32).astype(F32)
    notes = code[:, width:]
    first, second, third = notes[:, 1:2], notes[:, 2:3], notes[:, 3:4]
    proof = (first + (second + third * (1.0 / 32768.0)) * (1.0 / 32768.0)) * (1.0 / 8192.0)
    return code[:, :width] * (step_scale(notes[:, :1]) * (1.0 / LEVELS)), proof


def place(z):
    return z % 2 * 4 + z // 2


def handed_on(arrays, *awaited):
    there = pl.BlockSpec(memory_space=pl.ANY)
    return pl.pallas_call(
        lambda *refs: None,
        out_shape=[shape(a.shape, a.dtype) for a in arrays],
        in_specs=[there] * (len(arrays) + len(awaited)),
        out_specs=[there] * len(arrays),
        input_output_aliases={i: i for i in range(len(arrays))},
        compiler_params=pltpu.CompilerParams(vmem_limit_bytes=4 << 20),
        name="handed_on",
    )(*arrays, *awaited)


def up_the_ring(x, step):
    ring = lax.axis_size(RING)
    return lax.ppermute(x, RING, [(place(i), place((i + step) % ring)) for i in range(ring)])


def along_line(x, shift, phase):
    pairs = []
    for i in range(4):
        for j in range(4):
            for c in range(2):
                there = (shift(i), j) if (c + phase) % 2 == 0 else (i, shift(j))
                pairs.append(((i * 2 + c) * 4 + j, (there[0] * 2 + c) * 4 + there[1]))
    return lax.ppermute(x, PLANE, pairs)


def line(x, phase):
    return [x] + [along_line(x, lambda i, k=k: (i + k) % 4, phase) for k in (1, 3, 2)]


def other_core(x):
    return lax.ppermute(x, "c", [(0, 1), (1, 0)])


def on_device(pool, targets, counts):
    ring = lax.axis_size(RING)
    height, width = pool.shape
    rows = ring * height
    target_count = float(height * lax.axis_size(AXES))

    block, chosen = in_vmem(
        pack_block,
        "pack_block",
        (shape((2 * height + META, width), BF16), shape((lax.axis_size(CHIPS), 1, LANES), F32)),
        limit=56,
    )(pool, targets, counts.reshape(1, height))
    chosen = lax.all_to_all(chosen, CHIPS, split_axis=0, concat_axis=0, tiled=True)
    blocks = line(block, 0)
    below, above = up_the_ring(pool, 1), up_the_ring(pool, ring - 1)
    pair = shape((5 * height // 2, width), BF16)
    piece, up_pair, down_pair = in_vmem(
        pack_line, "pack_line", (shape((2 * height * len(blocks) + META, width), BF16), pair, pair)
    )(*blocks, pool, below, above)
    pieces = line(piece, 1)
    pairs = up_the_ring(up_pair, 3), up_the_ring(down_pair, ring - 3)

    size = height * len(blocks)
    sums = (shape((rows, width), F32),) * 2 + (shape((rows, LANES), F32),) * 2

    def add(body, arrays, some, state, out_shape, aliases):
        return in_vmem(
            functools.partial(body, 256, len(some)),
            body.__name__,
            out_shape,
            flops=8 * rows * len(some) * size * width,
            scratch=[pltpu.VMEM((rows, len(some) * size), BF16)] * 2,
            limit=12,
            aliases=aliases,
        )(*arrays, *some, *state)

    def more(some, state):
        return add(more_columns, (panel, norms), some, state, sums, {2 + len(some) + i: i for i in range(4)})

    panel, norms, total, *state = add(
        first_columns,
        (pool, below, above, *pairs, chosen),
        pieces[:1],
        (),
        (shape((rows, width), BF16), shape((rows, LANES), F32), shape((8, LANES), F32), *sums),
        {},
    )
    totals = total, other_core(total)
    pieces = handed_on(pieces, norms)
    others = [other_core(p) for p in pieces]
    for some in (pieces[1:3], (pieces[3], others[0]), others[1:]):
        state = more(some, state)

    inputs = panel, *state, *totals
    whole, half = (shape((n, width + LANES), jnp.int16) for n in (2 * height, height // 2))
    up, down, up_half, down_half = in_vmem(
        functools.partial(far_terms, target_count, height),
        "far_terms",
        (whole, whole, half, half),
    )(*inputs)
    from_above, from_below = up_the_ring(down, ring - 1), up_the_ring(up, 1)
    half_above, half_below = up_the_ring(down_half, ring - 2), up_the_ring(up_half, 2)
    near = in_vmem(
        functools.partial(near_terms, target_count, height),
        "near_terms",
        (shape((3 * height, width), F32), shape((3 * height, LANES), F32)),
    )(*inputs)
    up, down = in_vmem(pass_on, "pass_on", (shape((height, width + LANES), jnp.int16),) * 2)(
        *near, from_below, from_above, half_below, half_above
    )
    far_above, far_below = up_the_ring(down, ring - 2), up_the_ring(up, 2)
    proof, gradient = in_vmem(
        add_up, "add_up", (shape((1, height), F32), shape((height, width), F32))
    )(*near, from_below, from_above, far_below, far_above)
    return proof.reshape(height), gradient


def solution(mesh):
    split = Mesh(mesh.devices.reshape(2, 4, 2, 4, 4), AXES)
    return jax.shard_map(
        on_device,
        mesh=split,
        in_specs=(P(AXES, None), P(AXES, None), P(AXES)),
        out_specs=(P(AXES), P(AXES, None)),
        check_vma=False,
    )
```

```python
import functools

import jax
import jax.numpy as jnp
from jax import lax
from jax.experimental import pallas as pl
from jax.experimental.pallas import tpu as pltpu
from jax.sharding import Mesh
from jax.sharding import PartitionSpec as P

AXES = ("zl", "x", "c", "y", "zh")
RING = ("zl", "zh")
CHIPS = ("zl", "x", "y", "zh")
PLANE = ("x", "c", "y")
LANES = 128
META = 16
LEVELS = 32767.0
OFFSETS = (3, 1, 5, 7, 4, 2, 6, 0)
F32, BF16 = jnp.float32, jnp.bfloat16


def shape(dims, dtype):
    return jax.ShapeDtypeStruct(dims, dtype)


def in_vmem(body, name, out_shape, flops=0, traffic=1 << 20, scratch=(), limit=12, aliases=None):
    spec = pl.BlockSpec(memory_space=pltpu.VMEM)

    def call(*args):
        return pl.pallas_call(
            body,
            out_shape=out_shape,
            in_specs=[spec] * len(args),
            out_specs=jax.tree.map(lambda _: spec, out_shape),
            scratch_shapes=scratch,
            compiler_params=pltpu.CompilerParams(vmem_limit_bytes=limit << 20),
            cost_estimate=pl.CostEstimate(flops=flops, bytes_accessed=traffic, transcendentals=0),
            input_output_aliases=aliases or {},
            name=name,
        )(*args)

    return call


def lane_sums(x):
    total = x[:, :LANES]
    for at in range(LANES, x.shape[1], LANES):
        total = total + x[:, at : at + LANES]
    return total


def square_norms(block):
    wide = block.astype(F32)
    return jnp.sum(lane_sums(wide * wide), axis=1, keepdims=True)


def along_lanes(column):
    return jnp.transpose(jnp.broadcast_to(column, (column.shape[0], LANES)))[:1]


def halves(a, b):
    return jnp.concatenate([a, b], axis=1)


def pack_block(pool, targets, counts, block, chosen):
    height = pool.shape[0]
    chosen[...] = jnp.full(chosen.shape, jnp.sum(counts[...].astype(F32)), F32)
    block[:height, :] = pool[...]
    block[height : 2 * height, :] = targets[...]
    norms = along_lanes(jnp.concatenate([square_norms(pool[...]), square_norms(targets[...])], axis=0))
    high = norms.astype(BF16).astype(F32)
    middle = (norms - high).astype(BF16).astype(F32)
    low = norms - high - middle
    weights = halves(counts[...].astype(F32), jnp.ones((1, height), F32))
    meta = jnp.concatenate([weights, high, middle, low, jnp.zeros((META - 4, LANES), F32)], axis=0)
    block[2 * height :, :] = jnp.concatenate(
        [meta, jnp.zeros((META, block.shape[1] - LANES), F32)], axis=1
    ).astype(BF16)


def pack_line(*refs):
    blocks, (own, below, above, chosen, piece, up_pair, down_pair, total) = refs[:-8], refs[-8:]
    total[...] = jnp.broadcast_to(jnp.sum(chosen[...], axis=0), total.shape)
    half = own.shape[0] // 2
    up_pair[...] = jnp.concatenate([own[...], above[...], below[:half, :]], axis=0)
    down_pair[...] = jnp.concatenate([own[...], below[...], above[half:, :]], axis=0)
    count, height = len(blocks), (blocks[0].shape[0] - META) // 2
    for j, block in enumerate(blocks):
        piece[j * height : (j + 1) * height, :] = block[:height, :]
        piece[(count + j) * height : (count + j + 1) * height, :] = block[height : 2 * height, :]
    metas = [block[2 * height :, :LANES].astype(F32) for block in blocks]
    lanes = [meta[:, half : half + height] for half in (0, height) for meta in metas]
    pairs = [halves(a, b) for a, b in zip(lanes[::2], lanes[1::2])]
    width = piece.shape[1] - LANES * len(pairs)
    piece[2 * count * height :, :] = jnp.concatenate(
        [*pairs, jnp.zeros((META, width), F32)], axis=1
    ).astype(BF16)


def add_columns(panel, norms, pieces, old, pulls, masses, weights, rows):
    height, width = panel.shape
    size = (pieces[0].shape[0] - META) // 2
    for half in range(2):
        for i, piece in enumerate(pieces):
            columns = piece[half * size : (half + 1) * size, :]
            meta = piece[2 * size :, half * size : (half + 1) * size].astype(F32)
            col_norms = meta[1:2] + meta[2:3] + meta[3:4]
            for at in range(0, height, rows):
                part = slice(at, at + rows)
                inner = lax.dot_general(
                    panel[part, :], columns, (((1,), (1,)), ((), ())), preferred_element_type=F32
                )
                squared = norms[part, :1] + col_norms - 2.0 * inner
                kernel = jnp.exp(-squared * (0.5 / width))
                if half == 0:
                    kernel = kernel * meta[:1]
                mass = lane_sums(kernel)
                if i > 0:
                    mass = masses[half][part, :] + mass
                elif old:
                    mass = old[2 + half][part, :] + mass
                masses[half][part, :] = mass
                weights[half][part, i * size : (i + 1) * size] = kernel.astype(BF16)
    for half in range(2):
        for at in range(0, height, rows):
            part = slice(at, at + rows)
            total = old[half][part, :] if old else None
            for i, piece in enumerate(pieces):
                one = jnp.dot(
                    weights[half][part, i * size : (i + 1) * size],
                    piece[half * size : (half + 1) * size, :],
                    preferred_element_type=F32,
                )
                total = one if total is None else total + one
            pulls[half][part, :] = total


def first_columns(rows, lines, own, below, above, far_below, far_above, *refs):
    pieces, refs = refs[:lines], refs[lines:]
    ordered, norms, pp, tp, pm, tm, *weights = refs
    height = own.shape[0]
    found = {
        0: own[...],
        1: above[...],
        7: below[...],
        3: far_above[:height, :],
        2: far_above[height : 2 * height, :],
        5: far_below[:height, :],
        6: far_below[height : 2 * height, :],
        4: jnp.concatenate([far_below[2 * height :, :], far_above[2 * height :, :]], axis=0),
    }
    for i, offset in enumerate(OFFSETS):
        part = slice(i * height, (i + 1) * height)
        block = found[offset]
        ordered[part, :] = block
        norms[part, :] = jnp.broadcast_to(square_norms(block), (height, LANES))
    add_columns(ordered, norms, pieces, (), (pp, tp), (pm, tm), weights, rows)


def more_columns(rows, lines, panel, norms, *refs):
    pieces, old, refs = refs[:lines], refs[lines : lines + 4], refs[lines + 4 :]
    pp, tp, pm, tm, *weights = refs
    add_columns(panel, norms, pieces, old, (pp, tp), (pm, tm), weights, rows)


def terms(target_count, panel, pp, tp, pm, tm, total, other_total, part):
    weight = total[:1, :1] + other_total[:1, :1]
    pool_mass = jnp.sum(pm[part, :], axis=1, keepdims=True)
    target_mass = jnp.sum(tm[part, :], axis=1, keepdims=True)
    own = panel[part, :].astype(F32)
    proof = target_mass / target_count - pool_mass / weight
    gradient = (tp[part, :] - target_mass * own) * (1.0 / target_count) - (
        pp[part, :] - pool_mass * own
    ) * (1.0 / weight)
    return gradient, proof


def last_columns(lines, start, stop, panel, norms, *refs):
    pieces, old, totals, outs = refs[:lines], refs[lines : lines + 4], refs[lines + 4 : lines + 6], refs[lines + 6 :]
    outs, (pp, tp, pm, tm, *weights) = outs[:-6], outs[-6:]
    rows = slice(start, stop)
    panel, norms, *old = (ref.at[rows] for ref in (panel, norms, *old))
    add_columns(panel, norms, pieces, old, (pp, tp), (pm, tm), weights, stop - start)
    return (panel, pp, tp, pm, tm, *totals), outs


def far_terms(target_count, lines, height, *refs):
    inputs, (up, down, up_half, down_half) = last_columns(lines, 0, 5 * height, *refs)
    for i in range(4):
        code = encode(*terms(target_count, *inputs, slice(i * height, (i + 1) * height)))
        (up, down)[i // 2][i % 2 * height : (i % 2 + 1) * height, :] = code
    code = encode(*terms(target_count, *inputs, slice(4 * height, 5 * height)))
    down_half[...] = code[: height // 2, :]
    up_half[...] = code[height // 2 :, :]


def near_terms(target_count, lines, height, *refs):
    inputs, (gradient, proof) = last_columns(lines, 5 * height, 8 * height, *refs)
    for i in range(3):
        part = slice(i * height, (i + 1) * height)
        gradient[part, :], small = terms(target_count, *inputs, part)
        proof[part, :] = jnp.broadcast_to(small, (height, LANES))


def pass_on(gradient, proof, from_below, from_above, half_below, half_above, up, down):
    width, height = gradient.shape[1], gradient.shape[0] // 3
    for i, near, half, out in ((0, from_below, half_below, up), (1, from_above, half_above, down)):
        part = slice(i * height, (i + 1) * height)
        near_gradient, near_proof = decode(near[:height, :], width)
        half_gradient, half_proof = decode(half[...], width)
        zeros = jnp.zeros((height // 2, width), F32), jnp.zeros((height // 2, 1), F32)
        both = [(half_gradient, zeros[0]), (half_proof, zeros[1])]
        if i == 0:
            both = [pair[::-1] for pair in both]
        half_gradient, half_proof = (jnp.concatenate(pair, axis=0) for pair in both)
        out[...] = encode(
            gradient[part, :] + near_gradient + half_gradient,
            proof[part, :1] + near_proof + half_proof,
        )


def add_up(gradient, proof, from_below, from_above, far_below, far_above, out_proof, out):
    width, height = gradient.shape[1], gradient.shape[0] // 3
    total, small = gradient[2 * height :, :], proof[2 * height :, :1]
    for coded in (from_below[height:, :], from_above[height:, :], far_below[...], far_above[...]):
        one, part = decode(coded, width)
        total, small = total + one, small + part
    out[...] = total
    out_proof[...] = along_lanes(small)


def step_scale(step):
    return jnp.exp2(step * (1.0 / 128.0))


def encode(term, proof):
    top = jnp.maximum(jnp.max(jnp.abs(term), axis=1, keepdims=True), 1e-30)
    step = jnp.ceil(jnp.log2(top) * 128.0)
    steps = jnp.round(term * (LEVELS / step_scale(step)))
    steps = jnp.clip(steps, -LEVELS, LEVELS)
    first = jnp.round(proof * 8192.0)
    rest = (proof * 8192.0 - first) * 32768.0
    second = jnp.round(rest)
    third = jnp.round((rest - second) * 32768.0)
    lane = lax.broadcasted_iota(jnp.int32, (term.shape[0], LANES), 1)
    notes = jnp.where(
        lane == 0, step, jnp.where(lane == 1, first, jnp.where(lane == 2, second, third))
    )
    return jnp.concatenate([steps, notes], axis=1).astype(jnp.int32).astype(jnp.int16)


def decode(coded, width):
    code = coded.astype(jnp.int32).astype(F32)
    notes = code[:, width:]
    first, second, third = notes[:, 1:2], notes[:, 2:3], notes[:, 3:4]
    proof = (first + (second + third * (1.0 / 32768.0)) * (1.0 / 32768.0)) * (1.0 / 8192.0)
    return code[:, :width] * (step_scale(notes[:, :1]) * (1.0 / LEVELS)), proof


def place(z):
    return z % 2 * 4 + z // 2


def handed_on(arrays, *awaited):
    there = pl.BlockSpec(memory_space=pl.ANY)
    return pl.pallas_call(
        lambda *refs: None,
        out_shape=[shape(a.shape, a.dtype) for a in arrays],
        in_specs=[there] * (len(arrays) + len(awaited)),
        out_specs=[there] * len(arrays),
        input_output_aliases={i: i for i in range(len(arrays))},
        compiler_params=pltpu.CompilerParams(vmem_limit_bytes=4 << 20),
        name="handed_on",
    )(*arrays, *awaited)


def up_the_ring(x, step):
    ring = lax.axis_size(RING)
    return lax.ppermute(x, RING, [(place(i), place((i + step) % ring)) for i in range(ring)])


def along_line(x, shift, phase):
    pairs = []
    for i in range(4):
        for j in range(4):
            for c in range(2):
                there = (shift(i), j) if (c + phase) % 2 == 0 else (i, shift(j))
                pairs.append(((i * 2 + c) * 4 + j, (there[0] * 2 + c) * 4 + there[1]))
    return lax.ppermute(x, PLANE, pairs)


def line(x, phase):
    return [x] + [along_line(x, lambda i, k=k: (i + k) % 4, phase) for k in (1, 3, 2)]


def other_core(x):
    return lax.ppermute(x, "c", [(0, 1), (1, 0)])


def on_device(pool, targets, counts):
    ring = lax.axis_size(RING)
    height, width = pool.shape
    rows = ring * height
    target_count = float(height * lax.axis_size(AXES))

    block, chosen = in_vmem(
        pack_block,
        "pack_block",
        (shape((2 * height + META, width), BF16), shape((lax.axis_size(CHIPS), 1, LANES), F32)),
        limit=56,
    )(pool, targets, counts.reshape(1, height))
    chosen = lax.all_to_all(chosen, CHIPS, split_axis=0, concat_axis=0, tiled=True)
    blocks = line(block, 0)
    below, above = up_the_ring(pool, 1), up_the_ring(pool, ring - 1)
    pair = shape((5 * height // 2, width), BF16)
    piece, up_pair, down_pair, total = in_vmem(
        pack_line,
        "pack_line",
        (shape((2 * height * len(blocks) + META, width), BF16), pair, pair, shape((8, LANES), F32)),
    )(*blocks, pool, below, above, chosen)
    pieces = line(piece, 1)
    pairs = up_the_ring(up_pair, 3), up_the_ring(down_pair, ring - 3)

    size = height * len(blocks)
    sums = (shape((rows, width), F32),) * 2 + (shape((rows, LANES), F32),) * 2

    def add(body, arrays, some, state, out_shape, aliases):
        return in_vmem(
            functools.partial(body, 256, len(some)),
            body.__name__,
            out_shape,
            flops=8 * rows * len(some) * size * width,
            scratch=[pltpu.VMEM((rows, len(some) * size), BF16)] * 2,
            limit=12,
            aliases=aliases,
        )(*arrays, *some, *state)

    def more(some, state):
        return add(more_columns, (panel, norms), some, state, sums, {2 + len(some) + i: i for i in range(4)})

    panel, norms, *state = add(
        first_columns,
        (pool, below, above, *pairs),
        pieces[:1],
        (),
        (shape((rows, width), BF16), shape((rows, LANES), F32), *sums),
        {},
    )
    totals = total, other_core(total)
    pieces = handed_on(pieces, norms)
    others = [other_core(p) for p in pieces]
    for some in (pieces[1:3], (pieces[3], others[0])):
        state = more(some, state)

    inputs = panel, norms, *others[1:], *state, *totals

    def last(body, count, out_shape):
        return in_vmem(
            functools.partial(body, target_count, 3, height),
            body.__name__,
            out_shape,
            flops=8 * count * 3 * size * width,
            scratch=[pltpu.VMEM((count, n), F32) for n in (width, width, LANES, LANES)]
            + [pltpu.VMEM((count, 3 * size), BF16)] * 2,
            limit=16,
        )(*inputs)

    whole, half = (shape((n, width + LANES), jnp.int16) for n in (2 * height, height // 2))
    up, down, up_half, down_half = last(far_terms, 5 * height, (whole, whole, half, half))
    from_above, from_below = up_the_ring(down, ring - 1), up_the_ring(up, 1)
    half_above, half_below = up_the_ring(down_half, ring - 2), up_the_ring(up_half, 2)
    near = last(
        near_terms, 3 * height, (shape((3 * height, width), F32), shape((3 * height, LANES), F32))
    )
    up, down = in_vmem(pass_on, "pass_on", (shape((height, width + LANES), jnp.int16),) * 2)(
        *near, from_below, from_above, half_below, half_above
    )
    far_above, far_below = up_the_ring(down, ring - 2), up_the_ring(up, 2)
    proof, gradient = in_vmem(
        add_up, "add_up", (shape((1, height), F32), shape((height, width), F32))
    )(*near, from_below, from_above, far_below, far_above)
    return proof.reshape(height), gradient


def solution(mesh):
    split = Mesh(mesh.devices.reshape(2, 4, 2, 4, 4), AXES)
    return jax.shard_map(
        on_device,
        mesh=split,
        in_specs=(P(AXES, None), P(AXES, None), P(AXES)),
        out_specs=(P(AXES), P(AXES, None)),
        check_vma=False,
    )
```

```python
import functools

import jax
import jax.numpy as jnp
from jax import lax
from jax.experimental import pallas as pl
from jax.experimental.pallas import tpu as pltpu
from jax.sharding import Mesh
from jax.sharding import PartitionSpec as P

AXES = ("zl", "x", "c", "y", "zh")
RING = ("zl", "zh")
CHIPS = ("zl", "x", "y", "zh")
PLANE = ("x", "c", "y")
LANES = 128
META = 16
LEVELS = 32767.0
OFFSETS = (3, 1, 5, 7, 4, 2, 6, 0)
F32, BF16 = jnp.float32, jnp.bfloat16


def shape(dims, dtype):
    return jax.ShapeDtypeStruct(dims, dtype)


def in_vmem(body, name, out_shape, flops=0, traffic=1 << 20, scratch=(), limit=12, aliases=None):
    spec = pl.BlockSpec(memory_space=pltpu.VMEM)

    def call(*args):
        return pl.pallas_call(
            body,
            out_shape=out_shape,
            in_specs=[spec] * len(args),
            out_specs=jax.tree.map(lambda _: spec, out_shape),
            scratch_shapes=scratch,
            compiler_params=pltpu.CompilerParams(vmem_limit_bytes=limit << 20),
            cost_estimate=pl.CostEstimate(flops=flops, bytes_accessed=traffic, transcendentals=0),
            input_output_aliases=aliases or {},
            name=name,
        )(*args)

    return call


def lane_sums(x):
    total = x[:, :LANES]
    for at in range(LANES, x.shape[1], LANES):
        total = total + x[:, at : at + LANES]
    return total


def square_norms(block):
    wide = block.astype(F32)
    return jnp.sum(lane_sums(wide * wide), axis=1, keepdims=True)


def along_lanes(column):
    return jnp.transpose(jnp.broadcast_to(column, (column.shape[0], LANES)))[:1]


def halves(a, b):
    return jnp.concatenate([a, b], axis=1)


def pack_block(pool, targets, counts, block, chosen):
    height = pool.shape[0]
    chosen[...] = jnp.full(chosen.shape, jnp.sum(counts[...].astype(F32)), F32)
    block[:height, :] = pool[...]
    block[height : 2 * height, :] = targets[...]
    norms = along_lanes(jnp.concatenate([square_norms(pool[...]), square_norms(targets[...])], axis=0))
    high = norms.astype(BF16).astype(F32)
    middle = (norms - high).astype(BF16).astype(F32)
    low = norms - high - middle
    weights = halves(counts[...].astype(F32), jnp.ones((1, height), F32))
    meta = jnp.concatenate([weights, high, middle, low, jnp.zeros((META - 4, LANES), F32)], axis=0)
    block[2 * height :, :] = jnp.concatenate(
        [meta, jnp.zeros((META, block.shape[1] - LANES), F32)], axis=1
    ).astype(BF16)


def pack_line(*refs):
    blocks, (below, above, piece, up_pair, down_pair) = refs[:-5], refs[-5:]
    own = blocks[0].at[: below.shape[0]]
    half = own.shape[0] // 2
    up_pair[...] = jnp.concatenate([own[...], above[...], below[:half, :]], axis=0)
    down_pair[...] = jnp.concatenate([own[...], below[...], above[half:, :]], axis=0)
    count, height = len(blocks), (blocks[0].shape[0] - META) // 2
    for j, block in enumerate(blocks):
        piece[j * height : (j + 1) * height, :] = block[:height, :]
        piece[(count + j) * height : (count + j + 1) * height, :] = block[height : 2 * height, :]
    metas = [block[2 * height :, :LANES].astype(F32) for block in blocks]
    lanes = [meta[:, half : half + height] for half in (0, height) for meta in metas]
    pairs = [halves(a, b) for a, b in zip(lanes[::2], lanes[1::2])]
    width = piece.shape[1] - LANES * len(pairs)
    piece[2 * count * height :, :] = jnp.concatenate(
        [*pairs, jnp.zeros((META, width), F32)], axis=1
    ).astype(BF16)


def add_columns(panel, norms, pieces, old, pulls, masses, weights, rows):
    height, width = panel.shape
    size = (pieces[0].shape[0] - META) // 2
    for half in range(2):
        for i, piece in enumerate(pieces):
            columns = piece[half * size : (half + 1) * size, :]
            meta = piece[2 * size :, half * size : (half + 1) * size].astype(F32)
            col_norms = meta[1:2] + meta[2:3] + meta[3:4]
            for at in range(0, height, rows):
                part = slice(at, at + rows)
                inner = lax.dot_general(
                    panel[part, :], columns, (((1,), (1,)), ((), ())), preferred_element_type=F32
                )
                squared = norms[part, :1] + col_norms - 2.0 * inner
                kernel = jnp.exp(-squared * (0.5 / width))
                if half == 0:
                    kernel = kernel * meta[:1]
                mass = lane_sums(kernel)
                if i > 0:
                    mass = masses[half][part, :] + mass
                elif old:
                    mass = old[2 + half][part, :] + mass
                masses[half][part, :] = mass
                weights[half][part, i * size : (i + 1) * size] = kernel.astype(BF16)
    for half in range(2):
        for at in range(0, height, rows):
            part = slice(at, at + rows)
            total = old[half][part, :] if old else None
            for i, piece in enumerate(pieces):
                one = jnp.dot(
                    weights[half][part, i * size : (i + 1) * size],
                    piece[half * size : (half + 1) * size, :],
                    preferred_element_type=F32,
                )
                total = one if total is None else total + one
            pulls[half][part, :] = total


def first_columns(rows, lines, block, below, above, far_below, far_above, chosen, *refs):
    pieces, refs = refs[:lines], refs[lines:]
    ordered, norms, total, pp, tp, pm, tm, *weights = refs
    total[...] = jnp.broadcast_to(jnp.sum(chosen[...], axis=0), total.shape)
    height = below.shape[0]
    found = {
        0: block[:height, :],
        1: above[...],
        7: below[...],
        3: far_above[:height, :],
        2: far_above[height : 2 * height, :],
        5: far_below[:height, :],
        6: far_below[height : 2 * height, :],
        4: jnp.concatenate([far_below[2 * height :, :], far_above[2 * height :, :]], axis=0),
    }
    for i, offset in enumerate(OFFSETS):
        part = slice(i * height, (i + 1) * height)
        block = found[offset]
        ordered[part, :] = block
        norms[part, :] = jnp.broadcast_to(square_norms(block), (height, LANES))
    add_columns(ordered, norms, pieces, (), (pp, tp), (pm, tm), weights, rows)


def more_columns(rows, lines, panel, norms, *refs):
    pieces, old, refs = refs[:lines], refs[lines : lines + 4], refs[lines + 4 :]
    pp, tp, pm, tm, *weights = refs
    add_columns(panel, norms, pieces, old, (pp, tp), (pm, tm), weights, rows)


def terms(target_count, panel, pp, tp, pm, tm, total, other_total, part):
    weight = total[:1, :1] + other_total[:1, :1]
    pool_mass = jnp.sum(pm[part, :], axis=1, keepdims=True)
    target_mass = jnp.sum(tm[part, :], axis=1, keepdims=True)
    own = panel[part, :].astype(F32)
    proof = target_mass / target_count - pool_mass / weight
    gradient = (tp[part, :] - target_mass * own) * (1.0 / target_count) - (
        pp[part, :] - pool_mass * own
    ) * (1.0 / weight)
    return gradient, proof


def last_columns(lines, start, stop, panel, norms, *refs):
    pieces, old, totals, outs = refs[:lines], refs[lines : lines + 4], refs[lines + 4 : lines + 6], refs[lines + 6 :]
    outs, (pp, tp, pm, tm, *weights) = outs[:-6], outs[-6:]
    rows = slice(start, stop)
    panel, norms, *old = (ref.at[rows] for ref in (panel, norms, *old))
    add_columns(panel, norms, pieces, old, (pp, tp), (pm, tm), weights, stop - start)
    return (panel, pp, tp, pm, tm, *totals), outs


def far_terms(target_count, lines, height, *refs):
    inputs, (up, down, up_half, down_half) = last_columns(lines, 0, 5 * height, *refs)
    for i in range(4):
        code = encode(*terms(target_count, *inputs, slice(i * height, (i + 1) * height)))
        (up, down)[i // 2][i % 2 * height : (i % 2 + 1) * height, :] = code
    code = encode(*terms(target_count, *inputs, slice(4 * height, 5 * height)))
    down_half[...] = code[: height // 2, :]
    up_half[...] = code[height // 2 :, :]


def near_terms(target_count, lines, height, *refs):
    inputs, (gradient, proof) = last_columns(lines, 5 * height, 8 * height, *refs)
    for i in range(3):
        part = slice(i * height, (i + 1) * height)
        gradient[part, :], small = terms(target_count, *inputs, part)
        proof[part, :] = jnp.broadcast_to(small, (height, LANES))


def pass_on(gradient, proof, from_below, from_above, half_below, half_above, up, down):
    width, height = gradient.shape[1], gradient.shape[0] // 3
    for i, near, half, out in ((0, from_below, half_below, up), (1, from_above, half_above, down)):
        part = slice(i * height, (i + 1) * height)
        near_gradient, near_proof = decode(near[:height, :], width)
        half_gradient, half_proof = decode(half[...], width)
        zeros = jnp.zeros((height // 2, width), F32), jnp.zeros((height // 2, 1), F32)
        both = [(half_gradient, zeros[0]), (half_proof, zeros[1])]
        if i == 0:
            both = [pair[::-1] for pair in both]
        half_gradient, half_proof = (jnp.concatenate(pair, axis=0) for pair in both)
        out[...] = encode(
            gradient[part, :] + near_gradient + half_gradient,
            proof[part, :1] + near_proof + half_proof,
        )


def add_up(gradient, proof, from_below, from_above, far_below, far_above, out_proof, out):
    width, height = gradient.shape[1], gradient.shape[0] // 3
    total, small = gradient[2 * height :, :], proof[2 * height :, :1]
    for coded in (from_below[height:, :], from_above[height:, :], far_below[...], far_above[...]):
        one, part = decode(coded, width)
        total, small = total + one, small + part
    out[...] = total
    out_proof[...] = along_lanes(small)


def step_scale(step):
    return jnp.exp2(step * (1.0 / 128.0))


def encode(term, proof):
    top = jnp.maximum(jnp.max(jnp.abs(term), axis=1, keepdims=True), 1e-30)
    step = jnp.ceil(jnp.log2(top) * 128.0)
    steps = jnp.round(term * (LEVELS / step_scale(step)))
    steps = jnp.clip(steps, -LEVELS, LEVELS)
    first = jnp.round(proof * 8192.0)
    rest = (proof * 8192.0 - first) * 32768.0
    second = jnp.round(rest)
    third = jnp.round((rest - second) * 32768.0)
    lane = lax.broadcasted_iota(jnp.int32, (term.shape[0], LANES), 1)
    notes = jnp.where(
        lane == 0, step, jnp.where(lane == 1, first, jnp.where(lane == 2, second, third))
    )
    return jnp.concatenate([steps, notes], axis=1).astype(jnp.int32).astype(jnp.int16)


def decode(coded, width):
    code = coded.astype(jnp.int32).astype(F32)
    notes = code[:, width:]
    first, second, third = notes[:, 1:2], notes[:, 2:3], notes[:, 3:4]
    proof = (first + (second + third * (1.0 / 32768.0)) * (1.0 / 32768.0)) * (1.0 / 8192.0)
    return code[:, :width] * (step_scale(notes[:, :1]) * (1.0 / LEVELS)), proof


def place(z):
    return z % 2 * 4 + z // 2


def handed_on(arrays, *awaited):
    there = pl.BlockSpec(memory_space=pl.ANY)
    return pl.pallas_call(
        lambda *refs: None,
        out_shape=[shape(a.shape, a.dtype) for a in arrays],
        in_specs=[there] * (len(arrays) + len(awaited)),
        out_specs=[there] * len(arrays),
        input_output_aliases={i: i for i in range(len(arrays))},
        compiler_params=pltpu.CompilerParams(vmem_limit_bytes=4 << 20),
        name="handed_on",
    )(*arrays, *awaited)


def up_the_ring(x, step):
    ring = lax.axis_size(RING)
    return lax.ppermute(x, RING, [(place(i), place((i + step) % ring)) for i in range(ring)])


def along_line(x, shift, phase):
    pairs = []
    for i in range(4):
        for j in range(4):
            for c in range(2):
                there = (shift(i), j) if (c + phase) % 2 == 0 else (i, shift(j))
                pairs.append(((i * 2 + c) * 4 + j, (there[0] * 2 + c) * 4 + there[1]))
    return lax.ppermute(x, PLANE, pairs)


def line(x, phase):
    return [x] + [along_line(x, lambda i, k=k: (i + k) % 4, phase) for k in (1, 3, 2)]


def other_core(x):
    return lax.ppermute(x, "c", [(0, 1), (1, 0)])


def on_device(pool, targets, counts):
    ring = lax.axis_size(RING)
    height, width = pool.shape
    rows = ring * height
    target_count = float(height * lax.axis_size(AXES))

    block, chosen = in_vmem(
        pack_block,
        "pack_block",
        (shape((2 * height + META, width), BF16), shape((lax.axis_size(CHIPS), 1, LANES), F32)),
        limit=56,
    )(pool, targets, counts.reshape(1, height))
    chosen = lax.all_to_all(chosen, CHIPS, split_axis=0, concat_axis=0, tiled=True)
    blocks = line(block, 0)
    below, above = up_the_ring(pool, 1), up_the_ring(pool, ring - 1)
    pair = shape((5 * height // 2, width), BF16)
    piece, up_pair, down_pair = in_vmem(
        pack_line, "pack_line", (shape((2 * height * len(blocks) + META, width), BF16), pair, pair)
    )(*blocks, below, above)
    pieces = line(piece, 1)
    pairs = up_the_ring(up_pair, 3), up_the_ring(down_pair, ring - 3)

    size = height * len(blocks)
    sums = (shape((rows, width), F32),) * 2 + (shape((rows, LANES), F32),) * 2

    def add(body, arrays, some, state, out_shape, aliases):
        return in_vmem(
            functools.partial(body, 256, len(some)),
            body.__name__,
            out_shape,
            flops=8 * rows * len(some) * size * width,
            scratch=[pltpu.VMEM((rows, len(some) * size), BF16)] * 2,
            limit=12,
            aliases=aliases,
        )(*arrays, *some, *state)

    def more(some, state):
        return add(more_columns, (panel, norms), some, state, sums, {2 + len(some) + i: i for i in range(4)})

    panel, norms, total, *state = add(
        first_columns,
        (block, below, above, *pairs, chosen),
        pieces[:1],
        (),
        (shape((rows, width), BF16), shape((rows, LANES), F32), shape((8, LANES), F32), *sums),
        {},
    )
    totals = total, other_core(total)
    pieces = handed_on(pieces, norms)
    others = [other_core(p) for p in pieces]
    for some in (pieces[1:3], (pieces[3], others[0])):
        state = more(some, state)

    inputs = panel, norms, *others[1:], *state, *totals

    def last(body, count, out_shape):
        return in_vmem(
            functools.partial(body, target_count, 3, height),
            body.__name__,
            out_shape,
            flops=8 * count * 3 * size * width,
            scratch=[pltpu.VMEM((count, n), F32) for n in (width, width, LANES, LANES)]
            + [pltpu.VMEM((count, 3 * size), BF16)] * 2,
            limit=16,
        )(*inputs)

    whole, half = (shape((n, width + LANES), jnp.int16) for n in (2 * height, height // 2))
    up, down, up_half, down_half = last(far_terms, 5 * height, (whole, whole, half, half))
    from_above, from_below = up_the_ring(down, ring - 1), up_the_ring(up, 1)
    half_above, half_below = up_the_ring(down_half, ring - 2), up_the_ring(up_half, 2)
    near = last(
        near_terms, 3 * height, (shape((3 * height, width), F32), shape((3 * height, LANES), F32))
    )
    up, down = in_vmem(pass_on, "pass_on", (shape((height, width + LANES), jnp.int16),) * 2)(
        *near, from_below, from_above, half_below, half_above
    )
    far_above, far_below = up_the_ring(down, ring - 2), up_the_ring(up, 2)
    proof, gradient = in_vmem(
        add_up, "add_up", (shape((1, height), F32), shape((height, width), F32))
    )(*near, from_below, from_above, far_below, far_above)
    return proof.reshape(height), gradient


def solution(mesh):
    split = Mesh(mesh.devices.reshape(2, 4, 2, 4, 4), AXES)
    return jax.shard_map(
        on_device,
        mesh=split,
        in_specs=(P(AXES, None), P(AXES, None), P(AXES)),
        out_specs=(P(AXES), P(AXES, None)),
        check_vma=False,
    )
```

```python
import functools

import jax
import jax.numpy as jnp
from jax import lax
from jax.experimental import pallas as pl
from jax.experimental.pallas import tpu as pltpu
from jax.sharding import Mesh
from jax.sharding import PartitionSpec as P

AXES = ("zl", "x", "c", "y", "zh")
RING = ("zl", "zh")
CHIPS = ("zl", "x", "y", "zh")
PLANE = ("x", "c", "y")
LANES = 128
META = 16
LEVELS = 32767.0
OFFSETS = (3, 1, 5, 7, 4, 2, 6, 0)
F32, BF16 = jnp.float32, jnp.bfloat16


def shape(dims, dtype):
    return jax.ShapeDtypeStruct(dims, dtype)


def in_vmem(body, name, out_shape, flops=0, traffic=1 << 20, scratch=(), limit=12, aliases=None):
    spec = pl.BlockSpec(memory_space=pltpu.VMEM)

    def call(*args):
        return pl.pallas_call(
            body,
            out_shape=out_shape,
            in_specs=[spec] * len(args),
            out_specs=jax.tree.map(lambda _: spec, out_shape),
            scratch_shapes=scratch,
            compiler_params=pltpu.CompilerParams(vmem_limit_bytes=limit << 20),
            cost_estimate=pl.CostEstimate(flops=flops, bytes_accessed=traffic, transcendentals=0),
            input_output_aliases=aliases or {},
            name=name,
        )(*args)

    return call


def lane_sums(x):
    total = x[:, :LANES]
    for at in range(LANES, x.shape[1], LANES):
        total = total + x[:, at : at + LANES]
    return total


def square_norms(block):
    wide = block.astype(F32)
    return jnp.sum(lane_sums(wide * wide), axis=1, keepdims=True)


def along_lanes(column):
    return jnp.transpose(jnp.broadcast_to(column, (column.shape[0], LANES)))[:1]


def halves(a, b):
    return jnp.concatenate([a, b], axis=1)


def pack_block(pool, targets, counts, block, chosen):
    height = pool.shape[0]
    chosen[...] = jnp.full(chosen.shape, jnp.sum(counts[...].astype(F32)), F32)
    block[:height, :] = pool[...]
    block[height : 2 * height, :] = targets[...]
    norms = along_lanes(jnp.concatenate([square_norms(pool[...]), square_norms(targets[...])], axis=0))
    high = norms.astype(BF16).astype(F32)
    middle = (norms - high).astype(BF16).astype(F32)
    low = norms - high - middle
    weights = halves(counts[...].astype(F32), jnp.ones((1, height), F32))
    meta = jnp.concatenate([weights, high, middle, low, jnp.zeros((META - 4, LANES), F32)], axis=0)
    block[2 * height :, :] = jnp.concatenate(
        [meta, jnp.zeros((META, block.shape[1] - LANES), F32)], axis=1
    ).astype(BF16)


def pack_line(*refs):
    blocks, (below, above, piece, up_pair, down_pair) = refs[:-5], refs[-5:]
    own = blocks[0].at[: below.shape[0]]
    half = own.shape[0] // 2
    up_pair[...] = jnp.concatenate([own[...], above[...], below[:half, :]], axis=0)
    down_pair[...] = jnp.concatenate([own[...], below[...], above[half:, :]], axis=0)
    count, height = len(blocks), (blocks[0].shape[0] - META) // 2
    for j, block in enumerate(blocks):
        piece[j * height : (j + 1) * height, :] = block[:height, :]
        piece[(count + j) * height : (count + j + 1) * height, :] = block[height : 2 * height, :]
    metas = [block[2 * height :, :LANES].astype(F32) for block in blocks]
    lanes = [meta[:, half : half + height] for half in (0, height) for meta in metas]
    pairs = [halves(a, b) for a, b in zip(lanes[::2], lanes[1::2])]
    width = piece.shape[1] - LANES * len(pairs)
    piece[2 * count * height :, :] = jnp.concatenate(
        [*pairs, jnp.zeros((META, width), F32)], axis=1
    ).astype(BF16)


def add_columns(panel, norms, pieces, old, pulls, masses, weights, rows):
    height, width = panel.shape
    size = (pieces[0].shape[0] - META) // 2
    for half in range(2):
        for i, piece in enumerate(pieces):
            columns = piece[half * size : (half + 1) * size, :]
            meta = piece[2 * size :, half * size : (half + 1) * size].astype(F32)
            col_norms = meta[1:2] + meta[2:3] + meta[3:4]
            for at in range(0, height, rows):
                part = slice(at, at + rows)
                inner = lax.dot_general(
                    panel[part, :], columns, (((1,), (1,)), ((), ())), preferred_element_type=F32
                )
                squared = norms[part, :1] + col_norms - 2.0 * inner
                kernel = jnp.exp(-squared * (0.5 / width))
                if half == 0:
                    kernel = kernel * meta[:1]
                mass = lane_sums(kernel)
                if i > 0:
                    mass = masses[half][part, :] + mass
                elif old:
                    mass = old[2 + half][part, :] + mass
                masses[half][part, :] = mass
                weights[half][part, i * size : (i + 1) * size] = kernel.astype(BF16)
    for half in range(2):
        for at in range(0, height, rows):
            part = slice(at, at + rows)
            total = old[half][part, :] if old else None
            for i, piece in enumerate(pieces):
                one = jnp.dot(
                    weights[half][part, i * size : (i + 1) * size],
                    piece[half * size : (half + 1) * size, :],
                    preferred_element_type=F32,
                )
                total = one if total is None else total + one
            pulls[half][part, :] = total


def add_counts(chosen, total):
    total[...] = jnp.broadcast_to(jnp.sum(chosen[...], axis=0), total.shape)


def first_columns(rows, lines, block, below, above, far_below, far_above, *refs):
    pieces, refs = refs[:lines], refs[lines:]
    ordered, norms, pp, tp, pm, tm, *weights = refs
    height = below.shape[0]
    found = {
        0: block[:height, :],
        1: above[...],
        7: below[...],
        3: far_above[:height, :],
        2: far_above[height : 2 * height, :],
        5: far_below[:height, :],
        6: far_below[height : 2 * height, :],
        4: jnp.concatenate([far_below[2 * height :, :], far_above[2 * height :, :]], axis=0),
    }
    for i, offset in enumerate(OFFSETS):
        part = slice(i * height, (i + 1) * height)
        block = found[offset]
        ordered[part, :] = block
        norms[part, :] = jnp.broadcast_to(square_norms(block), (height, LANES))
    add_columns(ordered, norms, pieces, (), (pp, tp), (pm, tm), weights, rows)


def terms(target_count, panel, pp, tp, pm, tm, total, other_total, part):
    weight = total[:1, :1] + other_total[:1, :1]
    pool_mass = jnp.sum(pm[part, :], axis=1, keepdims=True)
    target_mass = jnp.sum(tm[part, :], axis=1, keepdims=True)
    own = panel[part, :].astype(F32)
    proof = target_mass / target_count - pool_mass / weight
    gradient = (tp[part, :] - target_mass * own) * (1.0 / target_count) - (
        pp[part, :] - pool_mass * own
    ) * (1.0 / weight)
    return gradient, proof


def last_columns(lines, start, stop, panel, norms, *refs):
    pieces, old, totals, outs = refs[:lines], refs[lines : lines + 4], refs[lines + 4 : lines + 6], refs[lines + 6 :]
    outs, (pp, tp, pm, tm, *weights) = outs[:-6], outs[-6:]
    rows = slice(start, stop)
    panel, norms, *old = (ref.at[rows] for ref in (panel, norms, *old))
    add_columns(panel, norms, pieces, old, (pp, tp), (pm, tm), weights, stop - start)
    return (panel, pp, tp, pm, tm, *totals), outs


def far_terms(target_count, lines, height, *refs):
    inputs, (up, down, up_half, down_half) = last_columns(lines, 0, 5 * height, *refs)
    for i in range(4):
        code = encode(*terms(target_count, *inputs, slice(i * height, (i + 1) * height)))
        (up, down)[i // 2][i % 2 * height : (i % 2 + 1) * height, :] = code
    code = encode(*terms(target_count, *inputs, slice(4 * height, 5 * height)))
    down_half[...] = code[: height // 2, :]
    up_half[...] = code[height // 2 :, :]


def near_terms(target_count, lines, height, *refs):
    inputs, (gradient, proof) = last_columns(lines, 5 * height, 8 * height, *refs)
    for i in range(3):
        part = slice(i * height, (i + 1) * height)
        gradient[part, :], small = terms(target_count, *inputs, part)
        proof[part, :] = jnp.broadcast_to(small, (height, LANES))


def pass_on(gradient, proof, from_below, from_above, half_below, half_above, up, down):
    width, height = gradient.shape[1], gradient.shape[0] // 3
    for i, near, half, out in ((0, from_below, half_below, up), (1, from_above, half_above, down)):
        part = slice(i * height, (i + 1) * height)
        near_gradient, near_proof = decode(near[:height, :], width)
        half_gradient, half_proof = decode(half[...], width)
        zeros = jnp.zeros((height // 2, width), F32), jnp.zeros((height // 2, 1), F32)
        both = [(half_gradient, zeros[0]), (half_proof, zeros[1])]
        if i == 0:
            both = [pair[::-1] for pair in both]
        half_gradient, half_proof = (jnp.concatenate(pair, axis=0) for pair in both)
        out[...] = encode(
            gradient[part, :] + near_gradient + half_gradient,
            proof[part, :1] + near_proof + half_proof,
        )


def add_up(gradient, proof, from_below, from_above, far_below, far_above, out_proof, out):
    width, height = gradient.shape[1], gradient.shape[0] // 3
    total, small = gradient[2 * height :, :], proof[2 * height :, :1]
    for coded in (from_below[height:, :], from_above[height:, :], far_below[...], far_above[...]):
        one, part = decode(coded, width)
        total, small = total + one, small + part
    out[...] = total
    out_proof[...] = along_lanes(small)


def step_scale(step):
    return jnp.exp2(step * (1.0 / 128.0))


def encode(term, proof):
    top = jnp.maximum(jnp.max(jnp.abs(term), axis=1, keepdims=True), 1e-30)
    step = jnp.ceil(jnp.log2(top) * 128.0)
    steps = jnp.round(term * (LEVELS / step_scale(step)))
    steps = jnp.clip(steps, -LEVELS, LEVELS)
    first = jnp.round(proof * 8192.0)
    rest = (proof * 8192.0 - first) * 32768.0
    second = jnp.round(rest)
    third = jnp.round((rest - second) * 32768.0)
    lane = lax.broadcasted_iota(jnp.int32, (term.shape[0], LANES), 1)
    notes = jnp.where(
        lane == 0, step, jnp.where(lane == 1, first, jnp.where(lane == 2, second, third))
    )
    return jnp.concatenate([steps, notes], axis=1).astype(jnp.int32).astype(jnp.int16)


def decode(coded, width):
    code = coded.astype(jnp.int32).astype(F32)
    notes = code[:, width:]
    first, second, third = notes[:, 1:2], notes[:, 2:3], notes[:, 3:4]
    proof = (first + (second + third * (1.0 / 32768.0)) * (1.0 / 32768.0)) * (1.0 / 8192.0)
    return code[:, :width] * (step_scale(notes[:, :1]) * (1.0 / LEVELS)), proof


def place(z):
    return z % 2 * 4 + z // 2


def handed_on(arrays, *awaited):
    there = pl.BlockSpec(memory_space=pl.ANY)
    return pl.pallas_call(
        lambda *refs: None,
        out_shape=[shape(a.shape, a.dtype) for a in arrays],
        in_specs=[there] * (len(arrays) + len(awaited)),
        out_specs=[there] * len(arrays),
        input_output_aliases={i: i for i in range(len(arrays))},
        compiler_params=pltpu.CompilerParams(vmem_limit_bytes=4 << 20),
        name="handed_on",
    )(*arrays, *awaited)


def up_the_ring(x, step):
    ring = lax.axis_size(RING)
    return lax.ppermute(x, RING, [(place(i), place((i + step) % ring)) for i in range(ring)])


def along_line(x, shift, phase):
    pairs = []
    for i in range(4):
        for j in range(4):
            for c in range(2):
                there = (shift(i), j) if (c + phase) % 2 == 0 else (i, shift(j))
                pairs.append(((i * 2 + c) * 4 + j, (there[0] * 2 + c) * 4 + there[1]))
    return lax.ppermute(x, PLANE, pairs)


def line(x, phase):
    return [x] + [along_line(x, lambda i, k=k: (i + k) % 4, phase) for k in (1, 3, 2)]


def other_core(x):
    return lax.ppermute(x, "c", [(0, 1), (1, 0)])


def on_device(pool, targets, counts):
    ring = lax.axis_size(RING)
    height, width = pool.shape
    rows = ring * height
    target_count = float(height * lax.axis_size(AXES))

    block, chosen = in_vmem(
        pack_block,
        "pack_block",
        (shape((2 * height + META, width), BF16), shape((lax.axis_size(CHIPS), 1, LANES), F32)),
        limit=56,
    )(pool, targets, counts.reshape(1, height))
    chosen = lax.all_to_all(chosen, CHIPS, split_axis=0, concat_axis=0, tiled=True)
    blocks = line(block, 0)
    below, above = up_the_ring(pool, 1), up_the_ring(pool, ring - 1)
    pair = shape((5 * height // 2, width), BF16)
    piece, up_pair, down_pair = in_vmem(
        pack_line, "pack_line", (shape((2 * height * len(blocks) + META, width), BF16), pair, pair)
    )(*blocks, below, above)
    pieces = line(piece, 1)
    pairs = up_the_ring(up_pair, 3), up_the_ring(down_pair, ring - 3)

    size = height * len(blocks)
    sums = (shape((rows, width), F32),) * 2 + (shape((rows, LANES), F32),) * 2

    def add(body, arrays, some, state, out_shape, aliases):
        return in_vmem(
            functools.partial(body, 256, len(some)),
            body.__name__,
            out_shape,
            flops=8 * rows * len(some) * size * width,
            scratch=[pltpu.VMEM((rows, len(some) * size), BF16)] * 2,
            limit=12,
            aliases=aliases,
        )(*arrays, *some, *state)

    pieces = handed_on(pieces, chosen, *pairs)
    total = in_vmem(add_counts, "add_counts", shape((8, LANES), F32))(chosen)
    others = [other_core(p) for p in pieces]
    panel, norms, *state = add(
        first_columns,
        (block, below, above, *pairs),
        pieces,
        (),
        (shape((rows, width), BF16), shape((rows, LANES), F32), *sums),
        {},
    )
    totals = total, other_core(total)
    inputs = panel, norms, *others, *state, *totals

    def last(body, count, out_shape):
        return in_vmem(
            functools.partial(body, target_count, len(others), height),
            body.__name__,
            out_shape,
            flops=8 * count * len(others) * size * width,
            scratch=[pltpu.VMEM((count, n), F32) for n in (width, width, LANES, LANES)]
            + [pltpu.VMEM((count, len(others) * size), BF16)] * 2,
            limit=16,
        )(*inputs)

    whole, half = (shape((n, width + LANES), jnp.int16) for n in (2 * height, height // 2))
    up, down, up_half, down_half = last(far_terms, 5 * height, (whole, whole, half, half))
    from_above, from_below = up_the_ring(down, ring - 1), up_the_ring(up, 1)
    half_above, half_below = up_the_ring(down_half, ring - 2), up_the_ring(up_half, 2)
    near = last(
        near_terms, 3 * height, (shape((3 * height, width), F32), shape((3 * height, LANES), F32))
    )
    up, down = in_vmem(pass_on, "pass_on", (shape((height, width + LANES), jnp.int16),) * 2)(
        *near, from_below, from_above, half_below, half_above
    )
    far_above, far_below = up_the_ring(down, ring - 2), up_the_ring(up, 2)
    proof, gradient = in_vmem(
        add_up, "add_up", (shape((1, height), F32), shape((height, width), F32))
    )(*near, from_below, from_above, far_below, far_above)
    return proof.reshape(height), gradient


def solution(mesh):
    split = Mesh(mesh.devices.reshape(2, 4, 2, 4, 4), AXES)
    return jax.shard_map(
        on_device,
        mesh=split,
        in_specs=(P(AXES, None), P(AXES, None), P(AXES)),
        out_specs=(P(AXES), P(AXES, None)),
        check_vma=False,
    )
```

```python
import functools

import jax
import jax.numpy as jnp
from jax import lax
from jax.experimental import pallas as pl
from jax.experimental.pallas import tpu as pltpu
from jax.sharding import Mesh
from jax.sharding import PartitionSpec as P

AXES = ("zl", "x", "c", "y", "zh")
RING = ("zl", "zh")
PLANE = ("x", "c", "y")
LANES = 128
META = 16
LEVELS = 32767.0
OFFSETS = (3, 1, 5, 7, 4, 2, 6, 0)
F32, BF16 = jnp.float32, jnp.bfloat16


def shape(dims, dtype):
    return jax.ShapeDtypeStruct(dims, dtype)


def in_vmem(body, name, out_shape, flops=0, traffic=1 << 20, scratch=(), limit=12, aliases=None):
    spec = pl.BlockSpec(memory_space=pltpu.VMEM)

    def call(*args):
        return pl.pallas_call(
            body,
            out_shape=out_shape,
            in_specs=[spec] * len(args),
            out_specs=jax.tree.map(lambda _: spec, out_shape),
            scratch_shapes=scratch,
            compiler_params=pltpu.CompilerParams(vmem_limit_bytes=limit << 20),
            cost_estimate=pl.CostEstimate(flops=flops, bytes_accessed=traffic, transcendentals=0),
            input_output_aliases=aliases or {},
            name=name,
        )(*args)

    return call


def lane_sums(x):
    total = x[:, :LANES]
    for at in range(LANES, x.shape[1], LANES):
        total = total + x[:, at : at + LANES]
    return total


def square_norms(block):
    wide = block.astype(F32)
    return jnp.sum(lane_sums(wide * wide), axis=1, keepdims=True)


def along_lanes(column):
    return jnp.transpose(jnp.broadcast_to(column, (column.shape[0], LANES)))[:1]


def halves(a, b):
    return jnp.concatenate([a, b], axis=1)


def pack_block(pool, targets, counts, block, chosen):
    height = pool.shape[0]
    chosen[...] = jnp.full(chosen.shape, jnp.sum(counts[...].astype(F32)), F32)
    block[:height, :] = pool[...]
    block[height : 2 * height, :] = targets[...]
    norms = along_lanes(jnp.concatenate([square_norms(pool[...]), square_norms(targets[...])], axis=0))
    high = norms.astype(BF16).astype(F32)
    middle = (norms - high).astype(BF16).astype(F32)
    low = norms - high - middle
    weights = halves(counts[...].astype(F32), jnp.ones((1, height), F32))
    meta = jnp.concatenate([weights, high, middle, low, jnp.zeros((META - 4, LANES), F32)], axis=0)
    block[2 * height :, :] = jnp.concatenate(
        [meta, jnp.zeros((META, block.shape[1] - LANES), F32)], axis=1
    ).astype(BF16)


def pack_line(*refs):
    blocks, (below, above, piece, up_pair, down_pair) = refs[:-5], refs[-5:]
    own = blocks[0].at[: below.shape[0]]
    half = own.shape[0] // 2
    up_pair[...] = jnp.concatenate([own[...], above[...], below[:half, :]], axis=0)
    down_pair[...] = jnp.concatenate([own[...], below[...], above[half:, :]], axis=0)
    count, height = len(blocks), (blocks[0].shape[0] - META) // 2
    for j, block in enumerate(blocks):
        piece[j * height : (j + 1) * height, :] = block[:height, :]
        piece[(count + j) * height : (count + j + 1) * height, :] = block[height : 2 * height, :]
    metas = [block[2 * height :, :LANES].astype(F32) for block in blocks]
    lanes = [meta[:, half : half + height] for half in (0, height) for meta in metas]
    pairs = [halves(a, b) for a, b in zip(lanes[::2], lanes[1::2])]
    width = piece.shape[1] - LANES * len(pairs)
    piece[2 * count * height :, :] = jnp.concatenate(
        [*pairs, jnp.zeros((META, width), F32)], axis=1
    ).astype(BF16)


def add_columns(panel, norms, pieces, old, pulls, masses, weights, rows):
    height, width = panel.shape
    size = (pieces[0].shape[0] - META) // 2
    for half in range(2):
        for i, piece in enumerate(pieces):
            columns = piece[half * size : (half + 1) * size, :]
            meta = piece[2 * size :, half * size : (half + 1) * size].astype(F32)
            col_norms = meta[1:2] + meta[2:3] + meta[3:4]
            for at in range(0, height, rows):
                part = slice(at, at + rows)
                inner = lax.dot_general(
                    panel[part, :], columns, (((1,), (1,)), ((), ())), preferred_element_type=F32
                )
                squared = norms[part, :1] + col_norms - 2.0 * inner
                kernel = jnp.exp(-squared * (0.5 / width))
                if half == 0:
                    kernel = kernel * meta[:1]
                mass = lane_sums(kernel)
                if i > 0:
                    mass = masses[half][part, :] + mass
                elif old:
                    mass = old[2 + half][part, :] + mass
                masses[half][part, :] = mass
                weights[half][part, i * size : (i + 1) * size] = kernel.astype(BF16)
    for half in range(2):
        for at in range(0, height, rows):
            part = slice(at, at + rows)
            total = old[half][part, :] if old else None
            for i, piece in enumerate(pieces):
                one = jnp.dot(
                    weights[half][part, i * size : (i + 1) * size],
                    piece[half * size : (half + 1) * size, :],
                    preferred_element_type=F32,
                )
                total = one if total is None else total + one
            pulls[half][part, :] = total


def add_counts(chosen, total):
    total[...] = jnp.broadcast_to(jnp.sum(chosen[...], axis=0), total.shape)


def first_columns(rows, lines, block, below, above, far_below, far_above, *refs):
    pieces, refs = refs[:lines], refs[lines:]
    ordered, norms, pp, tp, pm, tm, *weights = refs
    height = below.shape[0]
    found = {
        0: block[:height, :],
        1: above[...],
        7: below[...],
        3: far_above[:height, :],
        2: far_above[height : 2 * height, :],
        5: far_below[:height, :],
        6: far_below[height : 2 * height, :],
        4: jnp.concatenate([far_below[2 * height :, :], far_above[2 * height :, :]], axis=0),
    }
    for i, offset in enumerate(OFFSETS):
        part = slice(i * height, (i + 1) * height)
        block = found[offset]
        ordered[part, :] = block
        norms[part, :] = jnp.broadcast_to(square_norms(block), (height, LANES))
    add_columns(ordered, norms, pieces, (), (pp, tp), (pm, tm), weights, rows)


def terms(target_count, panel, pp, tp, pm, tm, total, part):
    weight = total[:1, :1]
    pool_mass = jnp.sum(pm[part, :], axis=1, keepdims=True)
    target_mass = jnp.sum(tm[part, :], axis=1, keepdims=True)
    own = panel[part, :].astype(F32)
    proof = target_mass / target_count - pool_mass / weight
    gradient = (tp[part, :] - target_mass * own) * (1.0 / target_count) - (
        pp[part, :] - pool_mass * own
    ) * (1.0 / weight)
    return gradient, proof


def last_columns(lines, start, stop, panel, norms, *refs):
    pieces, old, total, outs = refs[:lines], refs[lines : lines + 4], refs[lines + 4], refs[lines + 5 :]
    outs, (pp, tp, pm, tm, *weights) = outs[:-6], outs[-6:]
    rows = slice(start, stop)
    panel, norms, *old = (ref.at[rows] for ref in (panel, norms, *old))
    add_columns(panel, norms, pieces, old, (pp, tp), (pm, tm), weights, stop - start)
    return (panel, pp, tp, pm, tm, total), outs


def far_terms(target_count, lines, height, *refs):
    inputs, (up, down, up_half, down_half) = last_columns(lines, 0, 5 * height, *refs)
    for i in range(4):
        code = encode(*terms(target_count, *inputs, slice(i * height, (i + 1) * height)))
        (up, down)[i // 2][i % 2 * height : (i % 2 + 1) * height, :] = code
    code = encode(*terms(target_count, *inputs, slice(4 * height, 5 * height)))
    down_half[...] = code[: height // 2, :]
    up_half[...] = code[height // 2 :, :]


def near_terms(target_count, lines, height, *refs):
    inputs, (gradient, proof) = last_columns(lines, 5 * height, 8 * height, *refs)
    for i in range(3):
        part = slice(i * height, (i + 1) * height)
        gradient[part, :], small = terms(target_count, *inputs, part)
        proof[part, :] = jnp.broadcast_to(small, (height, LANES))


def pass_on(gradient, proof, from_below, from_above, half_below, half_above, up, down):
    width, height = gradient.shape[1], gradient.shape[0] // 3
    for i, near, half, out in ((0, from_below, half_below, up), (1, from_above, half_above, down)):
        part = slice(i * height, (i + 1) * height)
        near_gradient, near_proof = decode(near[:height, :], width)
        half_gradient, half_proof = decode(half[...], width)
        zeros = jnp.zeros((height // 2, width), F32), jnp.zeros((height // 2, 1), F32)
        both = [(half_gradient, zeros[0]), (half_proof, zeros[1])]
        if i == 0:
            both = [pair[::-1] for pair in both]
        half_gradient, half_proof = (jnp.concatenate(pair, axis=0) for pair in both)
        out[...] = encode(
            gradient[part, :] + near_gradient + half_gradient,
            proof[part, :1] + near_proof + half_proof,
        )


def add_up(gradient, proof, from_below, from_above, far_below, far_above, out_proof, out):
    width, height = gradient.shape[1], gradient.shape[0] // 3
    total, small = gradient[2 * height :, :], proof[2 * height :, :1]
    for coded in (from_below[height:, :], from_above[height:, :], far_below[...], far_above[...]):
        one, part = decode(coded, width)
        total, small = total + one, small + part
    out[...] = total
    out_proof[...] = along_lanes(small)


def step_scale(step):
    return jnp.exp2(step * (1.0 / 128.0))


def encode(term, proof):
    top = jnp.maximum(jnp.max(jnp.abs(term), axis=1, keepdims=True), 1e-30)
    step = jnp.ceil(jnp.log2(top) * 128.0)
    steps = jnp.round(term * (LEVELS / step_scale(step)))
    steps = jnp.clip(steps, -LEVELS, LEVELS)
    first = jnp.round(proof * 8192.0)
    rest = (proof * 8192.0 - first) * 32768.0
    second = jnp.round(rest)
    third = jnp.round((rest - second) * 32768.0)
    lane = lax.broadcasted_iota(jnp.int32, (term.shape[0], LANES), 1)
    notes = jnp.where(
        lane == 0, step, jnp.where(lane == 1, first, jnp.where(lane == 2, second, third))
    )
    return jnp.concatenate([steps, notes], axis=1).astype(jnp.int32).astype(jnp.int16)


def decode(coded, width):
    code = coded.astype(jnp.int32).astype(F32)
    notes = code[:, width:]
    first, second, third = notes[:, 1:2], notes[:, 2:3], notes[:, 3:4]
    proof = (first + (second + third * (1.0 / 32768.0)) * (1.0 / 32768.0)) * (1.0 / 8192.0)
    return code[:, :width] * (step_scale(notes[:, :1]) * (1.0 / LEVELS)), proof


def place(z):
    return z % 2 * 4 + z // 2


def handed_on(arrays, *awaited):
    there = pl.BlockSpec(memory_space=pl.ANY)
    return pl.pallas_call(
        lambda *refs: None,
        out_shape=[shape(a.shape, a.dtype) for a in arrays],
        in_specs=[there] * (len(arrays) + len(awaited)),
        out_specs=[there] * len(arrays),
        input_output_aliases={i: i for i in range(len(arrays))},
        compiler_params=pltpu.CompilerParams(vmem_limit_bytes=4 << 20),
        name="handed_on",
    )(*arrays, *awaited)


def up_the_ring(x, step):
    ring = lax.axis_size(RING)
    return lax.ppermute(x, RING, [(place(i), place((i + step) % ring)) for i in range(ring)])


def along_line(x, shift, phase):
    pairs = []
    for i in range(4):
        for j in range(4):
            for c in range(2):
                there = (shift(i), j) if (c + phase) % 2 == 0 else (i, shift(j))
                pairs.append(((i * 2 + c) * 4 + j, (there[0] * 2 + c) * 4 + there[1]))
    return lax.ppermute(x, PLANE, pairs)


def line(x, phase):
    return [x] + [along_line(x, lambda i, k=k: (i + k) % 4, phase) for k in (1, 3, 2)]


def other_core(x):
    return lax.ppermute(x, "c", [(0, 1), (1, 0)])


def on_device(pool, targets, counts):
    ring = lax.axis_size(RING)
    height, width = pool.shape
    rows = ring * height
    target_count = float(height * lax.axis_size(AXES))

    block, chosen = in_vmem(
        pack_block,
        "pack_block",
        (shape((2 * height + META, width), BF16), shape((lax.axis_size(AXES), 1, LANES), F32)),
        limit=56,
    )(pool, targets, counts.reshape(1, height))
    chosen = lax.all_to_all(chosen, AXES, split_axis=0, concat_axis=0, tiled=True)
    blocks = line(block, 0)
    below, above = up_the_ring(pool, 1), up_the_ring(pool, ring - 1)
    pair = shape((5 * height // 2, width), BF16)
    piece, up_pair, down_pair = in_vmem(
        pack_line, "pack_line", (shape((2 * height * len(blocks) + META, width), BF16), pair, pair)
    )(*blocks, below, above)
    pieces = line(piece, 1)
    pairs = up_the_ring(up_pair, 3), up_the_ring(down_pair, ring - 3)

    size = height * len(blocks)
    sums = (shape((rows, width), F32),) * 2 + (shape((rows, LANES), F32),) * 2

    def add(body, arrays, some, state, out_shape, aliases):
        return in_vmem(
            functools.partial(body, 256, len(some)),
            body.__name__,
            out_shape,
            flops=8 * rows * len(some) * size * width,
            scratch=[pltpu.VMEM((rows, len(some) * size), BF16)] * 2,
            limit=12,
            aliases=aliases,
        )(*arrays, *some, *state)

    pieces = handed_on(pieces, chosen, *pairs)
    total = in_vmem(add_counts, "add_counts", shape((8, LANES), F32))(chosen)
    others = [other_core(p) for p in pieces]
    panel, norms, *state = add(
        first_columns,
        (block, below, above, *pairs),
        pieces,
        (),
        (shape((rows, width), BF16), shape((rows, LANES), F32), *sums),
        {},
    )
    inputs = panel, norms, *others, *state, total

    def last(body, count, out_shape):
        return in_vmem(
            functools.partial(body, target_count, len(others), height),
            body.__name__,
            out_shape,
            flops=8 * count * len(others) * size * width,
            scratch=[pltpu.VMEM((count, n), F32) for n in (width, width, LANES, LANES)]
            + [pltpu.VMEM((count, len(others) * size), BF16)] * 2,
            limit=16,
        )(*inputs)

    whole, half = (shape((n, width + LANES), jnp.int16) for n in (2 * height, height // 2))
    up, down, up_half, down_half = last(far_terms, 5 * height, (whole, whole, half, half))
    from_above, from_below = up_the_ring(down, ring - 1), up_the_ring(up, 1)
    half_above, half_below = up_the_ring(down_half, ring - 2), up_the_ring(up_half, 2)
    near = last(
        near_terms, 3 * height, (shape((3 * height, width), F32), shape((3 * height, LANES), F32))
    )
    up, down = in_vmem(pass_on, "pass_on", (shape((height, width + LANES), jnp.int16),) * 2)(
        *near, from_below, from_above, half_below, half_above
    )
    far_above, far_below = up_the_ring(down, ring - 2), up_the_ring(up, 2)
    proof, gradient = in_vmem(
        add_up, "add_up", (shape((1, height), F32), shape((height, width), F32))
    )(*near, from_below, from_above, far_below, far_above)
    return proof.reshape(height), gradient


def solution(mesh):
    split = Mesh(mesh.devices.reshape(2, 4, 2, 4, 4), AXES)
    return jax.shard_map(
        on_device,
        mesh=split,
        in_specs=(P(AXES, None), P(AXES, None), P(AXES)),
        out_specs=(P(AXES), P(AXES, None)),
        check_vma=False,
    )
```

```python
import functools

import jax
import jax.numpy as jnp
from jax import lax
from jax.experimental import pallas as pl
from jax.experimental.pallas import tpu as pltpu
from jax.sharding import Mesh
from jax.sharding import PartitionSpec as P

AXES = ("zl", "x", "c", "y", "zh")
RING = ("zl", "zh")
CHIPS = ("zl", "x", "y", "zh")
PLANE = ("x", "c", "y")
LANES = 128
META = 16
LEVELS = 32767.0
OFFSETS = (3, 1, 5, 7, 4, 2, 6, 0)
F32, BF16 = jnp.float32, jnp.bfloat16


def shape(dims, dtype):
    return jax.ShapeDtypeStruct(dims, dtype)


def in_vmem(body, name, out_shape, flops=0, traffic=1 << 20, scratch=(), limit=12, aliases=None):
    spec = pl.BlockSpec(memory_space=pltpu.VMEM)

    def call(*args):
        return pl.pallas_call(
            body,
            out_shape=out_shape,
            in_specs=[spec] * len(args),
            out_specs=jax.tree.map(lambda _: spec, out_shape),
            scratch_shapes=scratch,
            compiler_params=pltpu.CompilerParams(vmem_limit_bytes=limit << 20),
            cost_estimate=pl.CostEstimate(flops=flops, bytes_accessed=traffic, transcendentals=0),
            input_output_aliases=aliases or {},
            name=name,
        )(*args)

    return call


def lane_sums(x):
    total = x[:, :LANES]
    for at in range(LANES, x.shape[1], LANES):
        total = total + x[:, at : at + LANES]
    return total


def square_norms(block):
    wide = block.astype(F32)
    return jnp.sum(lane_sums(wide * wide), axis=1, keepdims=True)


def along_lanes(column):
    return jnp.transpose(jnp.broadcast_to(column, (column.shape[0], LANES)))[:1]


def halves(a, b):
    return jnp.concatenate([a, b], axis=1)


def pack_block(pool, targets, counts, block, chosen):
    height = pool.shape[0]
    chosen[...] = jnp.full(chosen.shape, jnp.sum(counts[...].astype(F32)), F32)
    block[:height, :] = pool[...]
    block[height : 2 * height, :] = targets[...]
    norms = along_lanes(jnp.concatenate([square_norms(pool[...]), square_norms(targets[...])], axis=0))
    high = norms.astype(BF16).astype(F32)
    middle = (norms - high).astype(BF16).astype(F32)
    low = norms - high - middle
    weights = halves(counts[...].astype(F32), jnp.ones((1, height), F32))
    meta = jnp.concatenate([weights, high, middle, low, jnp.zeros((META - 4, LANES), F32)], axis=0)
    block[2 * height :, :] = jnp.concatenate(
        [meta, jnp.zeros((META, block.shape[1] - LANES), F32)], axis=1
    ).astype(BF16)


def pack_line(*refs):
    blocks, (below, above, piece, up_pair, down_pair) = refs[:-5], refs[-5:]
    own = blocks[0].at[: below.shape[0]]
    half = own.shape[0] // 2
    up_pair[...] = jnp.concatenate([own[...], above[...], below[:half, :]], axis=0)
    down_pair[...] = jnp.concatenate([own[...], below[...], above[half:, :]], axis=0)
    count, height = len(blocks), (blocks[0].shape[0] - META) // 2
    for j, block in enumerate(blocks):
        piece[j * height : (j + 1) * height, :] = block[:height, :]
        piece[(count + j) * height : (count + j + 1) * height, :] = block[height : 2 * height, :]
    metas = [block[2 * height :, :LANES].astype(F32) for block in blocks]
    lanes = [meta[:, half : half + height] for half in (0, height) for meta in metas]
    pairs = [halves(a, b) for a, b in zip(lanes[::2], lanes[1::2])]
    width = piece.shape[1] - LANES * len(pairs)
    piece[2 * count * height :, :] = jnp.concatenate(
        [*pairs, jnp.zeros((META, width), F32)], axis=1
    ).astype(BF16)


def add_columns(panel, norms, pieces, old, pulls, masses, weights, rows):
    height, width = panel.shape
    size = (pieces[0].shape[0] - META) // 2
    for half in range(2):
        for i, piece in enumerate(pieces):
            columns = piece[half * size : (half + 1) * size, :]
            meta = piece[2 * size :, half * size : (half + 1) * size].astype(F32)
            col_norms = meta[1:2] + meta[2:3] + meta[3:4]
            for at in range(0, height, rows):
                part = slice(at, at + rows)
                inner = lax.dot_general(
                    panel[part, :], columns, (((1,), (1,)), ((), ())), preferred_element_type=F32
                )
                squared = norms[part, :1] + col_norms - 2.0 * inner
                kernel = jnp.exp(-squared * (0.5 / width))
                if half == 0:
                    kernel = kernel * meta[:1]
                mass = lane_sums(kernel)
                if i > 0:
                    mass = masses[half][part, :] + mass
                elif old:
                    mass = old[2 + half][part, :] + mass
                masses[half][part, :] = mass
                weights[half][part, i * size : (i + 1) * size] = kernel.astype(BF16)
    for half in range(2):
        for at in range(0, height, rows):
            part = slice(at, at + rows)
            total = old[half][part, :] if old else None
            for i, piece in enumerate(pieces):
                one = jnp.dot(
                    weights[half][part, i * size : (i + 1) * size],
                    piece[half * size : (half + 1) * size, :],
                    preferred_element_type=F32,
                )
                total = one if total is None else total + one
            pulls[half][part, :] = total


def add_counts(chosen, total):
    total[...] = jnp.broadcast_to(jnp.sum(chosen[...], axis=0), total.shape)


def first_columns(rows, lines, block, below, above, far_below, far_above, *refs):
    pieces, refs = refs[:lines], refs[lines:]
    ordered, norms, pp, tp, pm, tm, *weights = refs
    height = below.shape[0]
    found = {
        0: block[:height, :],
        1: above[...],
        7: below[...],
        3: far_above[:height, :],
        2: far_above[height : 2 * height, :],
        5: far_below[:height, :],
        6: far_below[height : 2 * height, :],
        4: jnp.concatenate([far_below[2 * height :, :], far_above[2 * height :, :]], axis=0),
    }
    for i, offset in enumerate(OFFSETS):
        part = slice(i * height, (i + 1) * height)
        block = found[offset]
        ordered[part, :] = block
        norms[part, :] = jnp.broadcast_to(square_norms(block), (height, LANES))
    add_columns(ordered, norms, pieces, (), (pp, tp), (pm, tm), weights, rows)


def terms(target_count, panel, pp, tp, pm, tm, total, other_total, part):
    weight = total[:1, :1] + other_total[:1, :1]
    pool_mass = jnp.sum(pm[part, :], axis=1, keepdims=True)
    target_mass = jnp.sum(tm[part, :], axis=1, keepdims=True)
    own = panel[part, :].astype(F32)
    proof = target_mass / target_count - pool_mass / weight
    gradient = (tp[part, :] - target_mass * own) * (1.0 / target_count) - (
        pp[part, :] - pool_mass * own
    ) * (1.0 / weight)
    return gradient, proof


def last_columns(lines, start, stop, panel, norms, *refs):
    pieces, old, totals, outs = refs[:lines], refs[lines : lines + 4], refs[lines + 4 : lines + 6], refs[lines + 6 :]
    outs, (pp, tp, pm, tm, *weights) = outs[:-6], outs[-6:]
    rows = slice(start, stop)
    panel, norms, *old = (ref.at[rows] for ref in (panel, norms, *old))
    add_columns(panel, norms, pieces, old, (pp, tp), (pm, tm), weights, stop - start)
    return (panel, pp, tp, pm, tm, *totals), outs


def far_terms(target_count, lines, height, *refs):
    inputs, (up, down, across) = last_columns(lines, 0, 5 * height, *refs)
    for i in range(4):
        code = encode(*terms(target_count, *inputs, slice(i * height, (i + 1) * height)))
        (up, down)[i // 2][i % 2 * height : (i % 2 + 1) * height, :] = code
    across[...] = encode(*terms(target_count, *inputs, slice(4 * height, 5 * height)))


def near_terms(target_count, lines, height, *refs):
    inputs, (gradient, proof) = last_columns(lines, 5 * height, 8 * height, *refs)
    for i in range(3):
        part = slice(i * height, (i + 1) * height)
        gradient[part, :], small = terms(target_count, *inputs, part)
        proof[part, :] = jnp.broadcast_to(small, (height, LANES))


def pass_on(gradient, proof, from_below, from_above, up, down):
    width, height = gradient.shape[1], gradient.shape[0] // 3
    for i, near, out in ((0, from_below, up), (1, from_above, down)):
        part = slice(i * height, (i + 1) * height)
        near_gradient, near_proof = decode(near[:height, :], width)
        out[...] = encode(gradient[part, :] + near_gradient, proof[part, :1] + near_proof)


def add_up(gradient, proof, from_below, from_above, opposite, far_below, far_above, out_proof, out):
    width, height = gradient.shape[1], gradient.shape[0] // 3
    total, small = gradient[2 * height :, :], proof[2 * height :, :1]
    near = from_below[height:, :], from_above[height:, :]
    for coded in (*near, opposite[...], far_below[...], far_above[...]):
        one, part = decode(coded, width)
        total, small = total + one, small + part
    out[...] = total
    out_proof[...] = along_lanes(small)


def step_scale(step):
    return jnp.exp2(step * (1.0 / 128.0))


def encode(term, proof):
    top = jnp.maximum(jnp.max(jnp.abs(term), axis=1, keepdims=True), 1e-30)
    step = jnp.ceil(jnp.log2(top) * 128.0)
    steps = jnp.round(term * (LEVELS / step_scale(step)))
    steps = jnp.clip(steps, -LEVELS, LEVELS)
    first = jnp.round(proof * 8192.0)
    rest = (proof * 8192.0 - first) * 32768.0
    second = jnp.round(rest)
    third = jnp.round((rest - second) * 32768.0)
    lane = lax.broadcasted_iota(jnp.int32, (term.shape[0], LANES), 1)
    notes = jnp.where(
        lane == 0, step, jnp.where(lane == 1, first, jnp.where(lane == 2, second, third))
    )
    return jnp.concatenate([steps, notes], axis=1).astype(jnp.int32).astype(jnp.int16)


def decode(coded, width):
    code = coded.astype(jnp.int32).astype(F32)
    notes = code[:, width:]
    first, second, third = notes[:, 1:2], notes[:, 2:3], notes[:, 3:4]
    proof = (first + (second + third * (1.0 / 32768.0)) * (1.0 / 32768.0)) * (1.0 / 8192.0)
    return code[:, :width] * (step_scale(notes[:, :1]) * (1.0 / LEVELS)), proof


def place(z):
    return z % 2 * 4 + z // 2


def handed_on(arrays, *awaited):
    there = pl.BlockSpec(memory_space=pl.ANY)
    return pl.pallas_call(
        lambda *refs: None,
        out_shape=[shape(a.shape, a.dtype) for a in arrays],
        in_specs=[there] * (len(arrays) + len(awaited)),
        out_specs=[there] * len(arrays),
        input_output_aliases={i: i for i in range(len(arrays))},
        compiler_params=pltpu.CompilerParams(vmem_limit_bytes=4 << 20),
        name="handed_on",
    )(*arrays, *awaited)


def up_the_ring(x, step):
    ring = lax.axis_size(RING)
    return lax.ppermute(x, RING, [(place(i), place((i + step) % ring)) for i in range(ring)])


def along_line(x, shift, phase):
    pairs = []
    for i in range(4):
        for j in range(4):
            for c in range(2):
                there = (shift(i), j) if (c + phase) % 2 == 0 else (i, shift(j))
                pairs.append(((i * 2 + c) * 4 + j, (there[0] * 2 + c) * 4 + there[1]))
    return lax.ppermute(x, PLANE, pairs)


def line(x, phase):
    return [x] + [along_line(x, lambda i, k=k: (i + k) % 4, phase) for k in (1, 3, 2)]


def other_core(x):
    return lax.ppermute(x, "c", [(0, 1), (1, 0)])


def on_device(pool, targets, counts):
    ring = lax.axis_size(RING)
    height, width = pool.shape
    rows = ring * height
    target_count = float(height * lax.axis_size(AXES))

    block, chosen = in_vmem(
        pack_block,
        "pack_block",
        (shape((2 * height + META, width), BF16), shape((lax.axis_size(CHIPS), 1, LANES), F32)),
        limit=56,
    )(pool, targets, counts.reshape(1, height))
    chosen = lax.all_to_all(chosen, CHIPS, split_axis=0, concat_axis=0, tiled=True)
    blocks = line(block, 0)
    below, above = up_the_ring(pool, 1), up_the_ring(pool, ring - 1)
    pair = shape((5 * height // 2, width), BF16)
    piece, up_pair, down_pair = in_vmem(
        pack_line, "pack_line", (shape((2 * height * len(blocks) + META, width), BF16), pair, pair)
    )(*blocks, below, above)
    pieces = line(piece, 1)
    pairs = up_the_ring(up_pair, 3), up_the_ring(down_pair, ring - 3)

    size = height * len(blocks)
    sums = (shape((rows, width), F32),) * 2 + (shape((rows, LANES), F32),) * 2

    def add(body, arrays, some, state, out_shape, aliases):
        return in_vmem(
            functools.partial(body, 256, len(some)),
            body.__name__,
            out_shape,
            flops=8 * rows * len(some) * size * width,
            scratch=[pltpu.VMEM((rows, len(some) * size), BF16)] * 2,
            limit=12,
            aliases=aliases,
        )(*arrays, *some, *state)

    pieces = handed_on(pieces, chosen, *pairs)
    total = in_vmem(add_counts, "add_counts", shape((8, LANES), F32))(chosen)
    others = [other_core(p) for p in pieces]
    panel, norms, *state = add(
        first_columns,
        (block, below, above, *pairs),
        pieces,
        (),
        (shape((rows, width), BF16), shape((rows, LANES), F32), *sums),
        {},
    )
    totals = total, other_core(total)
    inputs = panel, norms, *others, *state, *totals

    def last(body, count, out_shape):
        return in_vmem(
            functools.partial(body, target_count, len(others), height),
            body.__name__,
            out_shape,
            flops=8 * count * len(others) * size * width,
            scratch=[pltpu.VMEM((count, n), F32) for n in (width, width, LANES, LANES)]
            + [pltpu.VMEM((count, len(others) * size), BF16)] * 2,
            limit=16,
        )(*inputs)

    two, one = (shape((n, width + LANES), jnp.int16) for n in (2 * height, height))
    up, down, across = last(far_terms, 5 * height, (two, two, one))
    from_above, from_below = up_the_ring(down, ring - 1), up_the_ring(up, 1)
    opposite = up_the_ring(across, ring // 2)
    near = last(
        near_terms, 3 * height, (shape((3 * height, width), F32), shape((3 * height, LANES), F32))
    )
    up, down = in_vmem(pass_on, "pass_on", (shape((height, width + LANES), jnp.int16),) * 2)(
        *near, from_below, from_above
    )
    far_above, far_below = up_the_ring(down, ring - 2), up_the_ring(up, 2)
    proof, gradient = in_vmem(
        add_up, "add_up", (shape((1, height), F32), shape((height, width), F32))
    )(*near, from_below, from_above, opposite, far_below, far_above)
    return proof.reshape(height), gradient


def solution(mesh):
    split = Mesh(mesh.devices.reshape(2, 4, 2, 4, 4), AXES)
    return jax.shard_map(
        on_device,
        mesh=split,
        in_specs=(P(AXES, None), P(AXES, None), P(AXES)),
        out_specs=(P(AXES), P(AXES, None)),
        check_vma=False,
    )
```
